256 devices in a mesh: hid: 64 (over y, z_hi, x), col: 4 (over z_lo, core).
Axes of the slice: x: 4, y: 4, z: 8 (z_hi: 4, z_lo: 2; z = z_hi * 2 + z_lo), core: 2. Of those that a mesh axis runs over, the one named last changes fastest.
Arguments:
- stream_a: bfloat16 [512, 8192], P('hid', 'col'), may hold values from -20 to 20
- stream_b: bfloat16 [512, 8192], P('hid', 'col'), may hold values from -20 to 20
- up_a: bfloat16 [8192, 28672], P('col', 'hid'), may hold values from -8 to 8
- up_b: bfloat16 [8192, 4, 7168], P('col', None, 'hid'), may hold values from -8 to 8
- gumbel: bfloat16 [28672, 28672], P('hid', 'col'), may hold values from -3 to 10
Outputs:
- row_pot: float32 [28672], P('hid')
- col_pot: float32 [4, 7168], P('col', 'hid')
The draws below stay inside these ranges and needn't reach their ends.
All inputs are finite; a program needn't handle non-finite values.
Results may differ from the reference program's by a relative error of at most 0.0068.
Values may be sent and summed in bfloat16 or wider, within the bound.
No kernel may reach another device: no remote copies, remote signals or barrier semaphores. Data moves between devices by JAX's collectives and lax.ppermute only.
A program may use at most 128 MiB of HBM per device.

```python
import math
import jax
import jax.numpy as jnp
from jax import lax

D = 8192
FF = 28672
ITERS = 3
TOKENS = 512
N_HID = 64
N_COL = 4


def scaled_rows(key, rows, cols):
    first, second = jax.random.split(key)
    values = jnp.clip(jax.random.normal(first, (rows, cols), jnp.float32), -6.0, 6.0)
    spread = jnp.exp(jax.random.uniform(second, (rows, 1), jnp.float32) * math.log(10.0))
    return values * spread / 3.0


def scaled_columns(key, rows, cols, reach):
    first, second = jax.random.split(key)
    values = jnp.clip(jax.random.normal(first, (rows, cols), jnp.float32), -6.0, 6.0)
    spread = jnp.exp(jax.random.uniform(second, (1, cols), jnp.float32) * math.log(reach))
    return values * spread / math.sqrt(rows * 1.0) / 2.0


def draw_stream_a(key, part):
    key = jax.random.fold_in(key, 11)
    return scaled_rows(key, TOKENS, D).astype(jnp.bfloat16)


def draw_stream_b(key, part):
    key = jax.random.fold_in(key, 12)
    return scaled_rows(key, TOKENS, D).astype(jnp.bfloat16)


def draw_up_a(key, part):
    key = jax.random.fold_in(key, 13)
    values = scaled_columns(key, D, FF, 10.0)
    return values.astype(jnp.bfloat16)


def draw_up_b(key, part):
    key = jax.random.fold_in(key, 14)
    values = scaled_columns(key, D, FF, 10.0)
    return values.reshape(D, N_COL, FF // N_COL).astype(jnp.bfloat16)


def draw_gumbel(key, part):
    key = jax.random.fold_in(key, 15)
    level = jax.random.uniform(key, (FF, FF), jnp.float32, 0.0001, 1.0 - 0.0001)
    values = -jnp.log(-jnp.log(level))
    return values.astype(jnp.bfloat16)


def setup_inputs(seed: int = 0) -> dict:
    key_list = jax.random.split(jax.random.key(seed), 6)
    stream_a = draw_stream_a(jax.random.fold_in(key_list[5], 71), 0)
    stream_b = draw_stream_b(jax.random.fold_in(key_list[5], 71), 0)
    up_a = draw_up_a(jax.random.fold_in(key_list[5], 71), 0)
    up_b = draw_up_b(jax.random.fold_in(key_list[5], 71), 0)
    gumbel = draw_gumbel(jax.random.fold_in(key_list[5], 71), 0)
    return {"stream_a": stream_a, "stream_b": stream_b, "up_a": up_a, "up_b": up_b, "gumbel": gumbel}


EPS = 1e-06
SHARPNESS = 32.0

def reference(stream_a, stream_b, up_a, up_b, gumbel):
    act_a = jnp.dot(stream_a, up_a, preferred_element_type=jnp.float32).astype(jnp.bfloat16)
    act_b = jnp.dot(stream_b, up_b.reshape(D, FF), preferred_element_type=jnp.float32).astype(jnp.bfloat16)
    fa = act_a.astype(jnp.float32)
    fb = act_b.astype(jnp.float32)
    inv_a = lax.rsqrt(lax.optimization_barrier(jnp.mean(fa * fa, axis=0)) + EPS)
    inv_b = lax.rsqrt(lax.optimization_barrier(jnp.mean(fb * fb, axis=0)) + EPS)
    block = FF // N_HID
    scale = SHARPNESS / TOKENS
    a_blocks = jnp.transpose(act_a.reshape(TOKENS, N_HID, block), (1, 0, 2))

    def make_rows(args):
        rows_a, scale_a, noise_rows = args
        cross = lax.dot_general(rows_a.astype(jnp.float32), fb, (((0,), (0,)), ((), ())), preferred_element_type=jnp.float32)
        return scale * cross * scale_a[:, None] * inv_b[None, :] + noise_rows.astype(jnp.float32)
    logits = lax.map(make_rows, (a_blocks, inv_a.reshape(N_HID, block), gumbel.reshape(N_HID, block, FF)))
    col_pot = jnp.zeros((FF,), jnp.float32)
    row_pot = jnp.zeros((FF,), jnp.float32)
    for step in range(ITERS):
        row_mass = lax.map(lambda rows: lax.optimization_barrier(jnp.sum(jnp.exp(rows + col_pot[None, :]), axis=1)), logits)
        row_pot = -jnp.log(row_mass.reshape(FF))
        row_blocks = row_pot.reshape(N_HID, block)
        col_terms = lax.map(lambda args: lax.optimization_barrier(jnp.sum(jnp.exp(args[0] + args[1][:, None]), axis=0)), (logits, row_blocks))
        col_pot = -jnp.log(lax.optimization_barrier(jnp.sum(col_terms, axis=0)))
    return (row_pot, col_pot.reshape(N_COL, FF // N_COL))
```

```python
import jax
import jax.numpy as jnp
from jax import lax
from jax.sharding import Mesh, PartitionSpec as P

ITERS = 3


EPS = 1e-06
SHARPNESS = 32.0

HID = ("y", "zh", "x")
COL = ("zl", "core")


def axis_sum(value, axis):
    size = lax.axis_size(axis)
    arrived = [
        lax.ppermute(value, axis, [(i, (i + shift) % size) for i in range(size)])
        for shift in range(1, size)
    ]
    for piece in arrived:
        value = value + piece
    return value


def hid_sum(value):
    for axis in ("x", "zh", "y"):
        value = axis_sum(value, axis)
    return value


def hid_gather(value, axis):
    for name in ("x", "zh", "y"):
        value = lax.all_gather(value, name, axis=axis, tiled=True)
    return value


def local(stream_a, stream_b, up_a, up_b, gumbel):
    tokens_b = hid_gather(stream_b, 0)
    tokens_a = hid_gather(stream_a, 0)
    count = tokens_a.shape[0]
    blocks = lax.axis_size(COL)
    part_a = jnp.dot(tokens_a, up_a, preferred_element_type=jnp.float32)
    flat_b = up_b.reshape(up_b.shape[0], -1)
    part_b = jnp.dot(tokens_b, flat_b, preferred_element_type=jnp.float32).reshape(
        count, blocks, -1
    )
    act_a = lax.psum(part_a, COL).astype(jnp.bfloat16)
    act_b = lax.psum_scatter(part_b, COL, scatter_dimension=1, tiled=True).astype(jnp.bfloat16)
    act_b = act_b.reshape(count, -1)
    float_a = act_a.astype(jnp.float32)
    inv_a = lax.rsqrt(jnp.mean(float_a * float_a, axis=0) + EPS)
    scale = SHARPNESS / count
    piece = hid_gather(act_b.T, 0).T
    float_b = piece.astype(jnp.float32)
    inv_b = lax.rsqrt(jnp.mean(float_b * float_b, axis=0) + EPS)
    cross = lax.dot_general(
        act_a, piece, (((0,), (0,)), ((), ())), preferred_element_type=jnp.float32
    )
    scores = scale * cross * inv_a[:, None] * inv_b[None, :]
    logits = scores + gumbel.astype(jnp.float32)
    width = logits.shape[1]
    share = width // lax.axis_size(HID)
    col_pot = jnp.zeros((width,), jnp.float32)
    row_pot = jnp.zeros((logits.shape[0],), jnp.float32)
    for step in range(ITERS):
        row_pot = -jnp.log(axis_sum(jnp.sum(jnp.exp(logits + col_pot[None, :]), axis=1), COL))
        partial_value = jnp.sum(jnp.exp(logits + row_pot[:, None]), axis=0)
        col_pot = -jnp.log(hid_sum(partial_value))
    own_share = lax.dynamic_slice_in_dim(col_pot, lax.axis_index(HID) * share, share)
    return (row_pot, own_share.reshape(1, share))


def solution(mesh):
    fine = Mesh(mesh.devices.reshape(4, 4, 4, 2, 2), HID + COL)
    placed = (
        P(HID, COL),
        P(HID, COL),
        P(COL, HID),
        P(COL, None, HID),
        P(HID, COL),
    )
    return jax.shard_map(
        local, mesh=fine, in_specs=placed, out_specs=(P(HID), P(COL, HID)), check_vma=False
    )
```

```python
import jax
import jax.numpy as jnp
from jax import lax
from jax.experimental import pallas as pl
from jax.experimental.pallas import tpu as pltpu
from jax.sharding import Mesh, PartitionSpec as P

ITERS = 3


EPS = 1e-06
SHARPNESS = 32.0

HID = ("y", "zh", "x")
COL = ("zl", "core")
TILE = 256


def shifted(value, axis):
    size = lax.axis_size(axis)
    return [value] + [
        lax.ppermute(value, axis, [(i, (i + shift) % size) for i in range(size)])
        for shift in range(1, size)
    ]


def crossed(value, axes):
    size = lax.axis_size(axes)
    return [value] + [
        lax.ppermute(value, axes, [(i, i ^ flip) for i in range(size)]) for flip in range(1, size)
    ]


def hid_sum(value):
    for axis in ("x", "zh", "y"):
        value = sum(shifted(value, axis))
    return value


def arrival_order(count, first, second):
    token = lax.broadcasted_iota(jnp.int32, (count, count), 1)
    arrived = lax.broadcasted_iota(jnp.int32, (count, count), 0)
    share = count // lax.axis_size(HID)
    place = {}
    rest = token // share
    for axis in ("x", "zh", "y"):
        size = lax.axis_size(axis)
        place[axis] = (lax.axis_index(axis) - rest % size + size) % size
        rest = rest // size
    row = (place[first] * lax.axis_size(second) + place[second]) * lax.axis_size("zh") + place["zh"]
    return (row * share + token % share == arrived).astype(jnp.bfloat16)


def scatter_sum(weights, tokens):
    depth, blocks, width = weights.shape
    weights = weights.reshape(depth, 2, 2, width)
    core = lax.axis_index("core")
    zl = lax.axis_index("zl")

    def product(which):
        part = lax.dynamic_index_in_dim(weights, which, axis=2, keepdims=False)
        part = part.reshape(depth, 2 * width)
        return lax.dot_general(
            part, tokens, (((0,), (1,)), ((), ())), preferred_element_type=jnp.float32
        ).reshape(2, width, -1)

    away = lax.ppermute(product(1 - core), "core", [(0, 1), (1, 0)])
    near = product(core) + away
    keep = jnp.where(zl == 0, near[0], near[1])
    give = jnp.where(zl == 0, near[1], near[0])
    return keep + lax.ppermute(give, "zl", [(0, 1), (1, 0)])


def plan_kernel(place, *refs):
    first, second, ours = refs[0:4], refs[4:8], refs[8:12]
    gumbel, plan, mass, held_b, held_a, inv_a, total, sem_b, sem_a = refs[12:]
    step = pl.program_id(0)
    rows, width = plan.shape
    half = first[0].shape[-1]
    y, x, c = place[0], place[1], place[2]

    def copies(block):
        found = []
        for s in range(4):
            for r in range(4):
                at_y = lax.rem(y - s + 4, 4)
                at_x = lax.rem(x - r + 4, 4)
                one = pltpu.make_async_copy(
                    first[s].at[r],
                    held_b.at[at_y, :, at_x, :, pl.ds(0, half)],
                    sem_b.at[at_y, r],
                )
                two = pltpu.make_async_copy(
                    second[r].at[s],
                    held_b.at[at_y, :, at_x, :, pl.ds(half, half)],
                    sem_b.at[at_y, 4 + r],
                )
                found += [one, two]
        return found

    @pl.when(step == 0)
    def _():
        moves = []
        for flip in range(4):
            moves.append(
                pltpu.make_async_copy(ours[flip], held_a.at[c ^ flip], sem_a.at[flip])
            )
        for move in moves:
            move.start()
        for move in copies(None):
            move.start()
        for move in moves:
            move.wait()
        values = held_a[...].reshape(rows, -1).astype(jnp.float32)
        scale = SHARPNESS / values.shape[1]
        inv_a[...] = scale * lax.rsqrt(jnp.mean(values * values, axis=1, keepdims=True) + EPS)
        total[...] = jnp.zeros_like(total)

    for r in range(4):
        pltpu.make_async_copy(
            first[0].at[r], held_b.at[step, :, 0, :, pl.ds(0, half)], sem_b.at[step, r]
        ).wait()
        pltpu.make_async_copy(
            second[0].at[r], held_b.at[step, :, 0, :, pl.ds(half, half)], sem_b.at[step, 4 + r]
        ).wait()

    left = held_a[...].reshape(rows, -1)
    flat = held_b.reshape(4 * width, left.shape[1])
    for tile in range(width // TILE):
        right = flat[pl.ds(pl.multiple_of(step * width + tile * TILE, TILE), TILE), :]
        cross = lax.dot_general(
            left, right, (((1,), (1,)), ((), ())), preferred_element_type=jnp.float32
        )
        spot = pl.ds(tile * TILE, TILE)
        value = jnp.exp(cross * inv_a[...] + gumbel[:, spot].astype(jnp.float32))
        plan[:, spot] = value
        total[...] += value[:, :128] + value[:, 128:]

    @pl.when(step == pl.num_programs(0) - 1)
    def _():
        mass[...] = jnp.sum(total[...], axis=1, keepdims=True)


def make_plan(first, second, ours, gumbel):
    rows, columns = gumbel.shape
    share, count = ours[0].shape
    width = columns // 4
    place = jnp.stack(
        [lax.axis_index("y"), lax.axis_index("x"), lax.axis_index(COL)]
    ).astype(jnp.int32)
    anywhere = pl.BlockSpec(memory_space=pl.ANY)
    return pl.pallas_call(
        plan_kernel,
        grid_spec=pltpu.PrefetchScalarGridSpec(
            num_scalar_prefetch=1,
            grid=(4,),
            in_specs=[anywhere] * 12 + [pl.BlockSpec((rows, width), lambda i, p: (0, i))],
            out_specs=[
                pl.BlockSpec((rows, width), lambda i, p: (0, i)),
                pl.BlockSpec((rows, 1), lambda i, p: (0, 0)),
            ],
            scratch_shapes=[
                pltpu.VMEM((4, 4, 4, share, count), jnp.bfloat16),
                pltpu.VMEM((4, share, count), jnp.bfloat16),
                pltpu.VMEM((rows, 1), jnp.float32),
                pltpu.VMEM((rows, 128), jnp.float32),
                pltpu.SemaphoreType.DMA((4, 8)),
                pltpu.SemaphoreType.DMA((4,)),
            ],
        ),
        out_shape=[
            jax.ShapeDtypeStruct((rows, columns), jnp.float32),
            jax.ShapeDtypeStruct((rows, 1), jnp.float32),
        ],
        compiler_params=pltpu.CompilerParams(
            dimension_semantics=("arbitrary",), vmem_limit_bytes=28 * 1024 * 1024
        ),
        cost_estimate=pl.CostEstimate(
            flops=2 * rows * columns * count,
            bytes_accessed=rows * columns * 6 + columns * count * 2,
            transcendentals=rows * columns,
        ),
    )(place, *first, *second, *ours, gumbel)


def local(stream_a, stream_b, up_a, up_b, gumbel):
    share = stream_a.shape[0]
    count = share * lax.axis_size(HID)
    near = shifted(jnp.concatenate([stream_a, stream_b], axis=0), "zh")
    near_a = jnp.concatenate([v[:share] for v in near], axis=0)
    near_b = jnp.concatenate([v[share:] for v in near], axis=0)
    near_b = jnp.concatenate(shifted(near_b, "x"), axis=0)
    near_a = jnp.concatenate(shifted(near_a, "y"), axis=0)
    tokens_b = jnp.concatenate(shifted(near_b, "y"), axis=0)
    tokens_a = jnp.concatenate(shifted(near_a, "x"), axis=0)

    act_b = scatter_sum(up_b, tokens_b).astype(jnp.bfloat16)
    act_b = jnp.dot(act_b, arrival_order(count, "y", "x"), preferred_element_type=jnp.float32)
    inv_b = lax.rsqrt(jnp.mean(act_b * act_b, axis=1, keepdims=True) + EPS)
    unit_b = (act_b * inv_b).astype(jnp.bfloat16)

    act_a = scatter_sum(up_a.reshape(up_a.shape[0], 4, -1), tokens_a).astype(jnp.bfloat16)
    act_a = jnp.dot(
        act_a, arrival_order(count, "x", "y"), preferred_element_type=jnp.float32
    ).astype(jnp.bfloat16)

    near = shifted(unit_b, "zh")
    me = lax.axis_index("zh")
    sorted_b = jnp.stack(
        [lax.select_n((me - z + 4) % 4, *near) for z in range(4)], axis=0
    )
    half = count // 2
    first = jnp.stack(shifted(sorted_b[:, :, :half], "x"), axis=0)
    second = jnp.stack(shifted(sorted_b[:, :, half:], "y"), axis=0)
    first = shifted(first, "y")
    second = shifted(second, "x")
    ours = crossed(act_a, COL)

    plan, mass = make_plan(first, second, ours, gumbel)
    row_mass = mass.reshape(-1)
    for step in range(ITERS):
        if step > 0:
            row_mass = jnp.sum(plan * (1.0 / col_mass)[None, :], axis=1)
        row_mass = sum(crossed(row_mass, COL))
        col_mass = hid_sum(jnp.sum(plan * (1.0 / row_mass)[:, None], axis=0))
    width = gumbel.shape[1] // lax.axis_size(HID)
    own = lax.dynamic_slice_in_dim(col_mass, lax.axis_index(HID) * width, width)
    return (-jnp.log(row_mass), -jnp.log(own).reshape(1, width))


def solution(mesh):
    fine = Mesh(mesh.devices.reshape(4, 4, 4, 2, 2), HID + COL)
    placed = (
        P(HID, COL),
        P(HID, COL),
        P(COL, HID),
        P(COL, None, HID),
        P(HID, COL),
    )
    return jax.shard_map(
        local, mesh=fine, in_specs=placed, out_specs=(P(HID), P(COL, HID)), check_vma=False
    )
```

```python
import jax
import jax.numpy as jnp
from jax import lax
from jax.experimental import pallas as pl
from jax.experimental.pallas import tpu as pltpu
from jax.sharding import Mesh, PartitionSpec as P

ITERS = 3


EPS = 1e-06
SHARPNESS = 32.0

HID = ("y", "zh", "x")
COL = ("zl", "core")
TILE = 256


def shifted(value, axis):
    size = lax.axis_size(axis)
    return [value] + [
        lax.ppermute(value, axis, [(i, (i + shift) % size) for i in range(size)])
        for shift in range(1, size)
    ]


def crossed(value, axes):
    size = lax.axis_size(axes)
    return [value] + [
        lax.ppermute(value, axes, [(i, i ^ flip) for i in range(size)]) for flip in range(1, size)
    ]


def hid_sum(value):
    for axis in ("x", "zh", "y"):
        value = sum(shifted(value, axis))
    return value


def in_order(near, axis):
    size = lax.axis_size(axis)
    me = lax.axis_index(axis)
    return jnp.stack(
        [lax.select_n((me - spot + size) % size, *near) for spot in range(size)], axis=0
    )


def project_kernel(place, *refs):
    near_a, near_b = refs[0:4], refs[4:8]
    weights_a, weights_b, mine, other, held_a, held_b, sem = refs[8:]
    y, x, zl, core = place[0], place[1], place[2], place[3]
    moves_a, moves_b = [], []
    for s in range(4):
        at_y = lax.rem(y - s + 4, 4)
        at_x = lax.rem(x - s + 4, 4)
        moves_a.append(pltpu.make_async_copy(near_a[s], held_a.at[:, at_x], sem.at[s]))
        moves_b.append(pltpu.make_async_copy(near_b[s], held_b.at[at_y], sem.at[4 + s]))
    for move in moves_b + moves_a:
        move.start()
    depth = held_a.shape[-1]
    for slot, moves, held, weights in ((0, moves_b, held_b, weights_b), (1, moves_a, held_a, weights_a)):
        for move in moves:
            move.wait()
        tokens = held[...].reshape(-1, depth)
        for out, which in ((other, 1 - core), (mine, core)):
            part = jnp.stack([weights[zl, which], weights[1 - zl, which]], axis=0)
            found = lax.dot_general(
                part.reshape(-1, depth),
                tokens,
                (((1,), (1,)), ((), ())),
                preferred_element_type=jnp.float32,
            )
            out[:, slot] = found.reshape(2, -1, found.shape[1])


def project(near_a, near_b, weights_a, weights_b):
    _, _, width, depth = weights_a.shape
    shape = near_a[0].shape
    count = 4 * shape[0] * shape[1]
    place = jnp.stack([lax.axis_index(axis) for axis in ("y", "x", "zl", "core")]).astype(jnp.int32)
    anywhere = pl.BlockSpec(memory_space=pl.ANY)
    inside = pl.BlockSpec(memory_space=pltpu.VMEM)
    out = jax.ShapeDtypeStruct((2, 2, width, count), jnp.float32)
    return pl.pallas_call(
        project_kernel,
        in_specs=[pl.BlockSpec(memory_space=pltpu.SMEM)] + [anywhere] * 8 + [inside] * 2,
        out_specs=[inside, inside],
        scratch_shapes=[
            pltpu.VMEM((4, 4) + shape[1:], jnp.bfloat16),
            pltpu.VMEM((4, 4) + shape[1:], jnp.bfloat16),
            pltpu.SemaphoreType.DMA((8,)),
        ],
        out_shape=[out, out],
        compiler_params=pltpu.CompilerParams(vmem_limit_bytes=20 * 1024 * 1024),
        cost_estimate=pl.CostEstimate(
            flops=2 * 8 * width * depth * count,
            bytes_accessed=(8 * width + 2 * count) * depth * 2,
            transcendentals=0,
        ),
    )(place, *near_a, *near_b, weights_a, weights_b)


def scatter_sum(mine, other):
    near = lax.ppermute(other, "core", [(0, 1), (1, 0)])
    away = lax.ppermute(mine[1] + near[1], "zl", [(0, 1), (1, 0)])
    return mine[0] + near[0] + away


def plan_kernel(place, *refs):
    first, second, ours = refs[0:4], refs[4:8], refs[8:12]
    noise, plan, mass, held_b, held_a, gumbel, inv_a, total, sem_b, sem_s, sem_a, sem_g = refs[12:]
    step = pl.program_id(0)
    rows, width = plan.shape
    half = first[0].shape[-1]
    y, x, c = place[0], place[1], place[2]

    def noise_move(block):
        spot = pl.ds(pl.multiple_of(block * width, width), width)
        return pltpu.make_async_copy(noise.at[:, spot], gumbel.at[block], sem_g.at[block])

    def first_move(s, block, spot):
        return pltpu.make_async_copy(
            first[s].at[spot],
            held_b.at[block, :, spot, :, pl.ds(0, half)],
            sem_b.at[block, spot],
        )

    def second_move(s):
        at_x = lax.rem(x - s + 4, 4)
        return pltpu.make_async_copy(
            second[s], held_b.at[:, :, at_x, :, pl.ds(half, half)], sem_s.at[s]
        )

    @pl.when(step == 0)
    def _():
        moves = [
            pltpu.make_async_copy(ours[flip], held_a.at[c ^ flip], sem_a.at[flip])
            for flip in range(4)
        ]
        later = [second_move(s) for s in range(4)]
        for move in moves:
            move.start()
        noise_move(0).start()
        for move in later:
            move.start()
        for s in range(4):
            for spot in range(4):
                first_move(s, lax.rem(y - s + 4, 4), spot).start()
        for block in range(1, 4):
            noise_move(block).start()
        for move in moves:
            move.wait()
        values = held_a[...].reshape(rows, -1).astype(jnp.float32)
        scale = SHARPNESS / values.shape[1]
        inv_a[...] = scale * lax.rsqrt(jnp.mean(values * values, axis=1, keepdims=True) + EPS)
        total[...] = jnp.zeros_like(total)
        for move in later:
            move.wait()

    for spot in range(4):
        first_move(0, step, spot).wait()
    noise_move(step).wait()
    left = held_a[...].reshape(rows, -1)
    flat = held_b.reshape(4 * width, left.shape[1])
    for tile in range(width // TILE):
        right = flat[pl.ds(pl.multiple_of(step * width + tile * TILE, TILE), TILE), :]
        cross = lax.dot_general(
            left, right, (((1,), (1,)), ((), ())), preferred_element_type=jnp.float32
        )
        square = right.astype(jnp.float32)
        square = square * square
        folded = square[:, :128]
        for lane in range(128, square.shape[1], 128):
            folded = folded + square[:, lane : lane + 128]
        power = lax.dot_general(
            jnp.full((8, 128), 1.0, jnp.float32),
            folded,
            (((1,), (1,)), ((), ())),
            precision=lax.Precision.HIGHEST,
            preferred_element_type=jnp.float32,
        )
        inv_b = lax.rsqrt(power[0:1, :] / square.shape[1] + EPS)
        spot = pl.ds(tile * TILE, TILE)
        noisy = gumbel[step, :, spot].astype(jnp.float32)
        value = jnp.exp(cross * inv_a[...] * inv_b + noisy)
        plan[:, spot] = value
        total[...] += value[:, :128] + value[:, 128:]

    @pl.when(step == pl.num_programs(0) - 1)
    def _():
        mass[...] = jnp.sum(total[...], axis=1, keepdims=True)


def make_plan(first, second, ours, gumbel):
    rows, columns = gumbel.shape
    share, count = ours[0].shape
    width = columns // 4
    place = jnp.stack(
        [lax.axis_index("y"), lax.axis_index("x"), lax.axis_index(COL)]
    ).astype(jnp.int32)
    anywhere = pl.BlockSpec(memory_space=pl.ANY)
    return pl.pallas_call(
        plan_kernel,
        grid_spec=pltpu.PrefetchScalarGridSpec(
            num_scalar_prefetch=1,
            grid=(4,),
            in_specs=[anywhere] * 12 + [pl.BlockSpec(memory_space=pltpu.HBM)],
            out_specs=[
                pl.BlockSpec((rows, width), lambda i, p: (0, i)),
                pl.BlockSpec((rows, 1), lambda i, p: (0, 0)),
            ],
            scratch_shapes=[
                pltpu.VMEM((4, 4, 4, share, count), jnp.bfloat16),
                pltpu.VMEM((4, share, count), jnp.bfloat16),
                pltpu.VMEM((4, rows, width), jnp.bfloat16),
                pltpu.VMEM((rows, 1), jnp.float32),
                pltpu.VMEM((rows, 128), jnp.float32),
                pltpu.SemaphoreType.DMA((4, 4)),
                pltpu.SemaphoreType.DMA((4,)),
                pltpu.SemaphoreType.DMA((4,)),
                pltpu.SemaphoreType.DMA((4,)),
            ],
        ),
        out_shape=[
            jax.ShapeDtypeStruct((rows, columns), jnp.float32),
            jax.ShapeDtypeStruct((rows, 1), jnp.float32),
        ],
        compiler_params=pltpu.CompilerParams(
            dimension_semantics=("arbitrary",), vmem_limit_bytes=26 * 1024 * 1024
        ),
        cost_estimate=pl.CostEstimate(
            flops=2 * rows * columns * count,
            bytes_accessed=rows * columns * 6 + columns * count * 2,
            transcendentals=rows * columns,
        ),
    )(place, *first, *second, *ours, gumbel)


def local(stream_a, stream_b, up_a, up_b, gumbel):
    share, depth = stream_a.shape
    half = share * lax.axis_size(HID) // 2
    up_a = up_a.T.reshape(2, 2, -1, depth)
    up_b = up_b.transpose(1, 2, 0).reshape(2, 2, -1, depth)

    which = lax.broadcasted_iota(jnp.int32, (2, share, depth), 0)
    near = shifted(jnp.where(which == 0, stream_a[None], stream_b[None]), "zh")
    near_a = in_order([v[0] for v in near], "zh").reshape(-1, depth)
    near_b = in_order([v[1] for v in near], "zh").reshape(-1, depth)
    near_b = in_order(shifted(near_b, "x"), "x")
    near_a = in_order(shifted(near_a, "y"), "y")
    near_b = shifted(near_b, "y")
    near_a = shifted(near_a, "x")
    acts = scatter_sum(*project(near_a, near_b, up_a, up_b)).astype(jnp.bfloat16)

    near = shifted(acts[0], "zh")
    first = in_order([v[:, :half] for v in near], "zh")
    second = in_order([v[:, half:] for v in near], "zh")
    first = in_order(shifted(first, "x"), "x")
    second = in_order(shifted(second, "y"), "y")
    first = shifted(first, "y")
    second = shifted(second, "x")
    ours = crossed(acts[1], COL)

    plan, mass = make_plan(first, second, ours, gumbel)
    row_mass = mass.reshape(-1)
    for step in range(ITERS):
        if step > 0:
            row_mass = jnp.sum(plan * (1.0 / col_mass)[None, :], axis=1)
        row_mass = sum(crossed(row_mass, COL))
        col_mass = hid_sum(jnp.sum(plan * (1.0 / row_mass)[:, None], axis=0))
    width = gumbel.shape[1] // lax.axis_size(HID)
    own = lax.dynamic_slice_in_dim(col_mass, lax.axis_index(HID) * width, width)
    return (-jnp.log(row_mass), -jnp.log(own).reshape(1, width))


def solution(mesh):
    fine = Mesh(mesh.devices.reshape(4, 4, 4, 2, 2), HID + COL)
    placed = (
        P(HID, COL),
        P(HID, COL),
        P(COL, HID),
        P(COL, None, HID),
        P(HID, COL),
    )
    return jax.shard_map(
        local, mesh=fine, in_specs=placed, out_specs=(P(HID), P(COL, HID)), check_vma=False
    )
```

```python
import jax
import jax.numpy as jnp
from jax import lax
from jax.experimental import pallas as pl
from jax.experimental.pallas import tpu as pltpu
from jax.sharding import Mesh, PartitionSpec as P

ITERS = 3


EPS = 1e-06
SHARPNESS = 32.0

HID = ("y", "zh", "x")
COL = ("zl", "core")
TILE = 256


def shifted(value, axis):
    size = lax.axis_size(axis)
    return [value] + [
        lax.ppermute(value, axis, [(i, (i + shift) % size) for i in range(size)])
        for shift in range(1, size)
    ]


def crossed(value, axes):
    size = lax.axis_size(axes)
    return [value] + [
        lax.ppermute(value, axes, [(i, i ^ flip) for i in range(size)]) for flip in range(1, size)
    ]


def turn():
    return 1 - 2 * lax.axis_index("core")


def spun(value, axis):
    size = lax.axis_size(axis)
    ahead = [(2 * i + c, 2 * ((i + 1 - 2 * c) % size) + c) for i in range(size) for c in (0, 1)]
    back = [(to, by) for by, to in ahead]
    one = lax.ppermute(value, (axis, "core"), ahead)
    three = lax.ppermute(value, (axis, "core"), back)
    two = lax.ppermute(one, (axis, "core"), ahead)
    return [value, one, two, three]


def together(one, one_axis, two, two_axis):
    one, two = lax.optimization_barrier((one, two))
    return lax.optimization_barrier((spun(one, one_axis), spun(two, two_axis)))


def hid_sum(value):
    for axis in ("x", "zh", "y"):
        value = sum(shifted(value, axis))
    return value


def in_order(near, axis, step=1):
    size = lax.axis_size(axis)
    me = lax.axis_index(axis)
    return jnp.stack(
        [lax.select_n(((me - spot) * step + size) % size, *near) for spot in range(size)], axis=0
    )


def project_kernel(place, *refs):
    near_a, near_b = refs[0:4], refs[4:8]
    up_a, up_b, mine, other, weights_a, weights_b, held_a, held_b, sem = refs[8:]
    y, x, zl, core, way = (place[i] for i in range(5))
    moves_a = [pltpu.make_async_copy(up_a, weights_a, sem.at[8])]
    moves_b = [pltpu.make_async_copy(up_b, weights_b, sem.at[9])]
    for s in range(4):
        at_y = lax.rem(y - s * way + 8, 4)
        at_x = lax.rem(x - s * way + 8, 4)
        moves_a.append(pltpu.make_async_copy(near_a[s], held_a.at[:, at_x], sem.at[s]))
        moves_b.append(pltpu.make_async_copy(near_b[s], held_b.at[at_y], sem.at[4 + s]))
    for move in moves_b + moves_a:
        move.start()
    depth = held_a.shape[-1]
    for slot, moves, held, weights in ((0, moves_b, held_b, weights_b), (1, moves_a, held_a, weights_a)):
        for move in moves:
            move.wait()
        tokens = held[...].reshape(-1, depth)
        for out, which in ((other, 1 - core), (mine, core)):
            part = jnp.stack([weights[zl, which], weights[1 - zl, which]], axis=0)
            found = lax.dot_general(
                part.reshape(-1, depth),
                tokens,
                (((1,), (1,)), ((), ())),
                preferred_element_type=jnp.float32,
            )
            out[:, slot] = found.reshape(2, -1, found.shape[1])


def project(near_a, near_b, weights_a, weights_b):
    _, _, width, depth = weights_a.shape
    shape = near_a[0].shape
    count = 4 * shape[0] * shape[1]
    place = [lax.axis_index(axis) for axis in ("y", "x", "zl", "core")] + [turn()]
    place = jnp.stack(place).astype(jnp.int32)
    anywhere = pl.BlockSpec(memory_space=pl.ANY)
    inside = pl.BlockSpec(memory_space=pltpu.VMEM)
    out = jax.ShapeDtypeStruct((2, 2, width, count), jnp.float32)
    return pl.pallas_call(
        project_kernel,
        in_specs=[pl.BlockSpec(memory_space=pltpu.SMEM)] + [anywhere] * 8 + [pl.BlockSpec(memory_space=pltpu.HBM)] * 2,
        out_specs=[inside, inside],
        scratch_shapes=[
            pltpu.VMEM(weights_a.shape, jnp.bfloat16),
            pltpu.VMEM(weights_b.shape, jnp.bfloat16),
            pltpu.VMEM((4, 4) + shape[1:], jnp.bfloat16),
            pltpu.VMEM((4, 4) + shape[1:], jnp.bfloat16),
            pltpu.SemaphoreType.DMA((10,)),
        ],
        out_shape=[out, out],
        compiler_params=pltpu.CompilerParams(vmem_limit_bytes=20 * 1024 * 1024),
        cost_estimate=pl.CostEstimate(
            flops=2 * 8 * width * depth * count,
            bytes_accessed=(8 * width + 2 * count) * depth * 2,
            transcendentals=0,
        ),
    )(place, *near_a, *near_b, weights_a, weights_b)


def scatter_sum(mine, other):
    near = lax.ppermute(other, "core", [(0, 1), (1, 0)])
    away = lax.ppermute(mine[1] + near[1], "zl", [(0, 1), (1, 0)])
    return mine[0] + near[0] + away


def plan_kernel(place, *refs):
    first, second, ours = refs[0:4], refs[4:8], refs[8:12]
    noise, plan, mass, held_b, held_a, gumbel, inv_a, total, sem_b, sem_s, sem_a, sem_g = refs[12:]
    step = pl.program_id(0)
    rows, columns = plan.shape
    width = columns // 4
    half = first[0].shape[-1]
    y, x, c, way = (place[i] for i in range(4))

    def noise_move(block):
        spot = pl.ds(pl.multiple_of(block * width, width), width)
        return pltpu.make_async_copy(noise.at[:, spot], gumbel.at[block], sem_g.at[block])

    def first_move(s, block, spot):
        return pltpu.make_async_copy(
            first[s].at[spot],
            held_b.at[block, :, spot, :, pl.ds(0, half)],
            sem_b.at[block, spot],
        )

    def second_move(s):
        at_x = lax.rem(x - s * way + 8, 4)
        return pltpu.make_async_copy(
            second[s], held_b.at[:, :, at_x, :, pl.ds(half, half)], sem_s.at[s]
        )

    @pl.when(step == 0)
    def _():
        moves = [
            pltpu.make_async_copy(ours[flip], held_a.at[c ^ flip], sem_a.at[flip])
            for flip in range(4)
        ]
        later = [second_move(s) for s in range(4)]
        for move in moves:
            move.start()
        noise_move(0).start()
        for move in later:
            move.start()
        for s in range(4):
            for spot in range(4):
                first_move(s, lax.rem(y - s * way + 8, 4), spot).start()
        for block in range(1, 4):
            noise_move(block).start()
        for move in moves:
            move.wait()
        values = held_a[...].reshape(rows, -1).astype(jnp.float32)
        scale = SHARPNESS / values.shape[1]
        inv_a[...] = scale * lax.rsqrt(jnp.mean(values * values, axis=1, keepdims=True) + EPS)
        total[...] = jnp.zeros_like(total)
        for move in later:
            move.wait()

    for spot in range(4):
        first_move(0, step, spot).wait()
    noise_move(step).wait()
    left = held_a[...].reshape(rows, -1)
    flat = held_b.reshape(4 * width, left.shape[1])
    for tile in range(width // TILE):
        right = flat[pl.ds(pl.multiple_of(step * width + tile * TILE, TILE), TILE), :]
        cross = lax.dot_general(
            left, right, (((1,), (1,)), ((), ())), preferred_element_type=jnp.float32
        )
        square = right.astype(jnp.float32)
        square = square * square
        folded = square[:, :128]
        for lane in range(128, square.shape[1], 128):
            folded = folded + square[:, lane : lane + 128]
        power = lax.dot_general(
            jnp.full((8, 128), 1.0, jnp.float32),
            folded,
            (((1,), (1,)), ((), ())),
            precision=lax.Precision.HIGHEST,
            preferred_element_type=jnp.float32,
        )
        inv_b = lax.rsqrt(power[0:1, :] / square.shape[1] + EPS)
        spot = pl.ds(tile * TILE, TILE)
        noisy = gumbel[step, :, spot].astype(jnp.float32)
        value = jnp.exp(cross * inv_a[...] * inv_b + noisy)
        plan[:, pl.ds(pl.multiple_of(step * width + tile * TILE, TILE), TILE)] = value
        total[...] += value[:, :128] + value[:, 128:]

    @pl.when(step == pl.num_programs(0) - 1)
    def _():
        mass[...] = jnp.sum(total[...], axis=1, keepdims=True)


def make_plan(first, second, ours, gumbel):
    rows, columns = gumbel.shape
    share, count = ours[0].shape
    width = columns // 4
    place = jnp.stack(
        [lax.axis_index("y"), lax.axis_index("x"), lax.axis_index(COL), turn()]
    ).astype(jnp.int32)
    return pl.pallas_call(
        plan_kernel,
        grid_spec=pltpu.PrefetchScalarGridSpec(
            num_scalar_prefetch=1,
            grid=(4,),
            in_specs=[pl.BlockSpec(memory_space=pltpu.HBM)] * 13,
            out_specs=[
                pl.BlockSpec(memory_space=pltpu.VMEM),
                pl.BlockSpec((rows, 1), lambda i, p: (0, 0)),
            ],
            scratch_shapes=[
                pltpu.VMEM((4, 4, 4, share, count), jnp.bfloat16),
                pltpu.VMEM((4, share, count), jnp.bfloat16),
                pltpu.VMEM((4, rows, width), jnp.bfloat16),
                pltpu.VMEM((rows, 1), jnp.float32),
                pltpu.VMEM((rows, 128), jnp.float32),
                pltpu.SemaphoreType.DMA((4, 4)),
                pltpu.SemaphoreType.DMA((4,)),
                pltpu.SemaphoreType.DMA((4,)),
                pltpu.SemaphoreType.DMA((4,)),
            ],
        ),
        out_shape=[
            pltpu.VMEM((rows, columns), jnp.float32),
            jax.ShapeDtypeStruct((rows, 1), jnp.float32),
        ],
        compiler_params=pltpu.CompilerParams(
            dimension_semantics=("arbitrary",), vmem_limit_bytes=26 * 1024 * 1024
        ),
        cost_estimate=pl.CostEstimate(
            flops=2 * rows * columns * count,
            bytes_accessed=rows * columns * 6 + columns * count * 2,
            transcendentals=rows * columns,
        ),
    )(place, *first, *second, *ours, gumbel)


def local(stream_a, stream_b, up_a, up_b, gumbel):
    share, depth = stream_a.shape
    half = share * lax.axis_size(HID) // 2
    up_a = up_a.T.reshape(2, 2, -1, depth)
    up_b = up_b.transpose(1, 2, 0).reshape(2, 2, -1, depth)

    which = lax.broadcasted_iota(jnp.int32, (2, share, depth), 0)
    near = shifted(jnp.where(which == 0, stream_a[None], stream_b[None]), "zh")
    near_a = in_order([v[0] for v in near], "zh").reshape(-1, depth)
    near_b = in_order([v[1] for v in near], "zh").reshape(-1, depth)
    near_b, near_a = together(near_b, "x", near_a, "y")
    near_b, near_a = in_order(near_b, "x", turn()), in_order(near_a, "y", turn())
    near_b, near_a = together(near_b, "y", near_a, "x")
    acts = scatter_sum(*project(near_a, near_b, up_a, up_b)).astype(jnp.bfloat16)

    near, mine = lax.optimization_barrier((shifted(acts[0], "zh"), acts[1]))
    first = in_order([v[:, :half] for v in near], "zh")
    second = in_order([v[:, half:] for v in near], "zh")
    first, second = together(first, "x", second, "y")
    first, second = in_order(first, "x", turn()), in_order(second, "y", turn())
    ours = crossed(mine, COL)
    first, second = together(first, "y", second, "x")

    plan, mass = make_plan(first, second, ours, gumbel)
    row_mass = mass.reshape(-1)
    for step in range(ITERS):
        if step > 0:
            row_mass = jnp.sum(plan * (1.0 / col_mass)[None, :], axis=1)
        row_mass = sum(crossed(row_mass, COL))
        col_mass = hid_sum(jnp.sum(plan * (1.0 / row_mass)[:, None], axis=0))
    width = gumbel.shape[1] // lax.axis_size(HID)
    own = lax.dynamic_slice_in_dim(col_mass, lax.axis_index(HID) * width, width)
    return (-jnp.log(row_mass), -jnp.log(own).reshape(1, width))


def solution(mesh):
    fine = Mesh(mesh.devices.reshape(4, 4, 4, 2, 2), HID + COL)
    placed = (
        P(HID, COL),
        P(HID, COL),
        P(COL, HID),
        P(COL, None, HID),
        P(HID, COL),
    )
    return jax.shard_map(
        local, mesh=fine, in_specs=placed, out_specs=(P(HID), P(COL, HID)), check_vma=False
    )
```

```python
import jax
import jax.numpy as jnp
from jax import lax
from jax.experimental import pallas as pl
from jax.experimental.pallas import tpu as pltpu
from jax.sharding import Mesh, PartitionSpec as P

ITERS = 3


EPS = 1e-06
SHARPNESS = 32.0

HID = ("y", "zh", "x")
COL = ("zl", "core")
TILE = 256


def shifted(value, axis):
    size = lax.axis_size(axis)
    return [value] + [
        lax.ppermute(value, axis, [(i, (i + shift) % size) for i in range(size)])
        for shift in range(1, size)
    ]


def crossed(value, axes):
    size = lax.axis_size(axes)
    return [value] + [
        lax.ppermute(value, axes, [(i, i ^ flip) for i in range(size)]) for flip in range(1, size)
    ]


def pinned(values):
    return [pltpu.with_memory_space_constraint(value, pltpu.HBM) for value in values]


def turn():
    return 1 - 2 * lax.axis_index("core")


def spun(value, axis):
    size = lax.axis_size(axis)
    ahead = [(2 * i + c, 2 * ((i + 1 - 2 * c) % size) + c) for i in range(size) for c in (0, 1)]
    back = [(to, by) for by, to in ahead]
    one = lax.ppermute(value, (axis, "core"), ahead)
    three = lax.ppermute(value, (axis, "core"), back)
    two = lax.ppermute(one, (axis, "core"), ahead)
    return [value, one, two, three]


def together(one, one_axis, two, two_axis):
    one, two = lax.optimization_barrier((one, two))
    return lax.optimization_barrier((spun(one, one_axis), spun(two, two_axis)))


def hid_sum(value):
    wide = jnp.broadcast_to(value, (16, value.shape[1]))
    value = jnp.sum(lax.all_to_all(wide, ("y", "x"), 0, 0, tiled=True), axis=0, keepdims=True)
    return sum(shifted(value, "zh"))


def hid_share(value):
    parts = value.reshape(lax.axis_size(HID), -1)
    return jnp.sum(lax.all_to_all(parts, HID, 0, 0, tiled=True), axis=0, keepdims=True)


def in_order(near, axis, step=1):
    size = lax.axis_size(axis)
    me = lax.axis_index(axis)
    return jnp.stack(
        [lax.select_n(((me - spot) * step + size) % size, *near) for spot in range(size)], axis=0
    )


def project_kernel(place, *refs):
    near_a, near_b = refs[0:4], refs[4:8]
    up_a, up_b, mine, other, weights_a, weights_b, held_a, held_b, sem = refs[8:]
    y, x, zl, core, way = (place[i] for i in range(5))
    moves_a = [pltpu.make_async_copy(up_a, weights_a, sem.at[8])]
    moves_b = [pltpu.make_async_copy(up_b, weights_b, sem.at[9])]
    for s in range(4):
        at_y = lax.rem(y - s * way + 8, 4)
        at_x = lax.rem(x - s * way + 8, 4)
        moves_a.append(pltpu.make_async_copy(near_a[s], held_a.at[:, at_x], sem.at[s]))
        moves_b.append(pltpu.make_async_copy(near_b[s], held_b.at[at_y], sem.at[4 + s]))
    for move in moves_b + moves_a:
        move.start()
    depth = held_a.shape[-1]
    for slot, moves, held, weights in ((0, moves_b, held_b, weights_b), (1, moves_a, held_a, weights_a)):
        for move in moves:
            move.wait()
        tokens = held[...].reshape(-1, depth)
        for out, which in ((other, 1 - core), (mine, core)):
            part = jnp.stack([weights[zl, which], weights[1 - zl, which]], axis=0)
            found = lax.dot_general(
                part.reshape(-1, depth),
                tokens,
                (((1,), (1,)), ((), ())),
                preferred_element_type=jnp.float32,
            )
            out[:, slot] = found.reshape(2, -1, found.shape[1])


def project(near_a, near_b, weights_a, weights_b):
    _, _, width, depth = weights_a.shape
    shape = near_a[0].shape
    count = 4 * shape[0] * shape[1]
    place = [lax.axis_index(axis) for axis in ("y", "x", "zl", "core")] + [turn()]
    place = jnp.stack(place).astype(jnp.int32)
    anywhere = pl.BlockSpec(memory_space=pl.ANY)
    inside = pl.BlockSpec(memory_space=pltpu.VMEM)
    out = jax.ShapeDtypeStruct((2, 2, width, count), jnp.float32)
    return pl.pallas_call(
        project_kernel,
        in_specs=[pl.BlockSpec(memory_space=pltpu.SMEM)] + [anywhere] * 8 + [pl.BlockSpec(memory_space=pltpu.HBM)] * 2,
        out_specs=[inside, inside],
        scratch_shapes=[
            pltpu.VMEM(weights_a.shape, jnp.bfloat16),
            pltpu.VMEM(weights_b.shape, jnp.bfloat16),
            pltpu.VMEM((4, 4) + shape[1:], jnp.bfloat16),
            pltpu.VMEM((4, 4) + shape[1:], jnp.bfloat16),
            pltpu.SemaphoreType.DMA((10,)),
        ],
        out_shape=[out, out],
        compiler_params=pltpu.CompilerParams(vmem_limit_bytes=20 * 1024 * 1024),
        cost_estimate=pl.CostEstimate(
            flops=2 * 8 * width * depth * count,
            bytes_accessed=(8 * width + 2 * count) * depth * 2,
            transcendentals=0,
        ),
    )(place, *near_a, *near_b, *pinned([weights_a, weights_b]))


def swapped(value, axis):
    return lax.ppermute(value, axis, [(0, 1), (1, 0)])


def padded(rows):
    return -(-rows // 128) * 128


def across(total):
    return jnp.sum(total[...].T, axis=0, keepdims=True)


def row_kernel(plan, col_mass, mass, scale, total):
    rows, columns = plan.shape
    scale[...] = 1.0 / col_mass[...]
    total[...] = jnp.zeros_like(total)

    def body(block, carry):
        spot = pl.ds(pl.multiple_of(block * 64, 64), 64)
        found = jnp.zeros((64, 128), jnp.float32)
        for lane in range(0, columns, 128):
            found = found + plan[spot, lane : lane + 128] * scale[:, lane : lane + 128]
        total[spot, :] = found
        return carry

    lax.fori_loop(0, rows // 64, body, 0)
    mass[...] = across(total)[:, :rows]


def col_kernel(plan, row_mass, mass, scale, wide):
    rows, columns = plan.shape
    scale[...] = jnp.ones_like(scale)
    scale[:, :rows] = 1.0 / row_mass[...]
    wide[...] = jnp.broadcast_to(scale[...], (128, scale.shape[1])).T

    def body(block, carry):
        spot = pl.ds(pl.multiple_of(block * 1024, 1024), 1024)
        found = jnp.zeros((8, 1024), jnp.float32)
        for row in range(0, rows, 8):
            factor = jnp.concatenate([wide[row : row + 8, :]] * 8, axis=1)
            found = found + plan[row : row + 8, spot] * factor
        mass[:, spot] = jnp.sum(found, axis=0, keepdims=True)
        return carry

    lax.fori_loop(0, columns // 1024, body, 0)


def plan_pass(kernel, plan, mass, width, scratch):
    inside = pl.BlockSpec(memory_space=pltpu.VMEM)
    return pl.pallas_call(
        kernel,
        in_specs=[inside, inside],
        out_specs=inside,
        out_shape=jax.ShapeDtypeStruct((1, width), jnp.float32),
        scratch_shapes=[pltpu.VMEM(shape, jnp.float32) for shape in scratch],
        compiler_params=pltpu.CompilerParams(vmem_limit_bytes=4 * 1024 * 1024),
        cost_estimate=pl.CostEstimate(
            flops=2 * plan.size, bytes_accessed=4 * plan.size, transcendentals=0
        ),
    )(pltpu.with_memory_space_constraint(plan, pltpu.VMEM), mass)


def row_sums(plan, col_mass):
    rows, columns = plan.shape
    return plan_pass(row_kernel, plan, col_mass, rows, [(1, columns), (padded(rows), 128)])


def col_sums(plan, row_mass):
    rows, columns = plan.shape
    return plan_pass(
        col_kernel, plan, row_mass, columns, [(1, padded(rows)), (padded(rows), 128)]
    )


def plan_kernel(place, *refs):
    first, second, ours = refs[0:4], refs[4:8], refs[8:12]
    noise, plan, mass, held_b, held_a, gumbel, inv_a, total, sem_b, sem_s, sem_a, sem_g = refs[12:]
    step = pl.program_id(0)
    rows, columns = plan.shape
    width = columns // 4
    half = first[0].shape[-1]
    y, x, c, way = (place[i] for i in range(4))

    def noise_move(block):
        spot = pl.ds(pl.multiple_of(block * width, width), width)
        return pltpu.make_async_copy(noise.at[:, spot], gumbel.at[block], sem_g.at[block])

    def first_move(s, block, spot):
        return pltpu.make_async_copy(
            first[s].at[spot],
            held_b.at[block, :, spot, :, pl.ds(0, half)],
            sem_b.at[block, spot],
        )

    def second_move(s):
        at_x = lax.rem(x - s * way + 8, 4)
        return pltpu.make_async_copy(
            second[s], held_b.at[:, :, at_x, :, pl.ds(half, half)], sem_s.at[s]
        )

    @pl.when(step == 0)
    def _():
        moves = [
            pltpu.make_async_copy(ours[flip], held_a.at[c ^ flip], sem_a.at[flip])
            for flip in range(4)
        ]
        later = [second_move(s) for s in range(4)]
        for move in moves:
            move.start()
        noise_move(0).start()
        for move in later:
            move.start()
        for s in range(4):
            for spot in range(4):
                first_move(s, lax.rem(y - s * way + 8, 4), spot).start()
        for block in range(1, 4):
            noise_move(block).start()
        for move in moves:
            move.wait()
        values = held_a[...].reshape(rows, -1).astype(jnp.float32)
        scale = SHARPNESS / values.shape[1]
        inv_a[...] = scale * lax.rsqrt(jnp.mean(values * values, axis=1, keepdims=True) + EPS)
        total[...] = jnp.zeros_like(total)
        for move in later:
            move.wait()

    for spot in range(4):
        first_move(0, step, spot).wait()
    noise_move(step).wait()
    left = held_a[...].reshape(rows, -1)
    flat = held_b.reshape(4 * width, left.shape[1])
    for tile in range(width // TILE):
        right = flat[pl.ds(pl.multiple_of(step * width + tile * TILE, TILE), TILE), :]
        cross = lax.dot_general(
            left, right, (((1,), (1,)), ((), ())), preferred_element_type=jnp.float32
        )
        square = right.astype(jnp.float32)
        square = square * square
        folded = square[:, :128]
        for lane in range(128, square.shape[1], 128):
            folded = folded + square[:, lane : lane + 128]
        power = lax.dot_general(
            jnp.full((8, 128), 1.0, jnp.float32),
            folded,
            (((1,), (1,)), ((), ())),
            precision=lax.Precision.HIGHEST,
            preferred_element_type=jnp.float32,
        )
        inv_b = lax.rsqrt(power[0:1, :] / square.shape[1] + EPS)
        spot = pl.ds(tile * TILE, TILE)
        noisy = gumbel[step, :, spot].astype(jnp.float32)
        value = jnp.exp(cross * inv_a[...] * inv_b + noisy)
        plan[:, pl.ds(pl.multiple_of(step * width + tile * TILE, TILE), TILE)] = value
        total[:rows, :] += value[:, :128] + value[:, 128:]

    @pl.when(step == pl.num_programs(0) - 1)
    def _():
        mass[...] = across(total)[:, :rows]


def make_plan(first, second, ours, gumbel):
    rows, columns = gumbel.shape
    share, count = ours[0].shape
    width = columns // 4
    place = jnp.stack(
        [lax.axis_index("y"), lax.axis_index("x"), lax.axis_index(COL), turn()]
    ).astype(jnp.int32)
    return pl.pallas_call(
        plan_kernel,
        grid_spec=pltpu.PrefetchScalarGridSpec(
            num_scalar_prefetch=1,
            grid=(4,),
            in_specs=[pl.BlockSpec(memory_space=pl.ANY)] * 12
            + [pl.BlockSpec(memory_space=pltpu.HBM)],
            out_specs=[
                pl.BlockSpec(memory_space=pltpu.VMEM),
                pl.BlockSpec((1, rows), lambda i, p: (0, 0)),
            ],
            scratch_shapes=[
                pltpu.VMEM((4, 4, 4, share, count), jnp.bfloat16),
                pltpu.VMEM((4, share, count), jnp.bfloat16),
                pltpu.VMEM((4, rows, width), jnp.bfloat16),
                pltpu.VMEM((rows, 1), jnp.float32),
                pltpu.VMEM((padded(rows), 128), jnp.float32),
                pltpu.SemaphoreType.DMA((4, 4)),
                pltpu.SemaphoreType.DMA((4,)),
                pltpu.SemaphoreType.DMA((4,)),
                pltpu.SemaphoreType.DMA((4,)),
            ],
        ),
        out_shape=[
            pltpu.VMEM((rows, columns), jnp.float32),
            jax.ShapeDtypeStruct((1, rows), jnp.float32),
        ],
        compiler_params=pltpu.CompilerParams(
            dimension_semantics=("arbitrary",), vmem_limit_bytes=26 * 1024 * 1024
        ),
        cost_estimate=pl.CostEstimate(
            flops=2 * rows * columns * count,
            bytes_accessed=rows * columns * 6 + columns * count * 2,
            transcendentals=rows * columns,
        ),
    )(place, *first, *second, *ours, *pinned([gumbel]))


def local(stream_a, stream_b, up_a, up_b, gumbel):
    share, depth = stream_a.shape
    half = share * lax.axis_size(HID) // 2
    up_a = up_a.T.reshape(2, 2, -1, depth)
    up_b = up_b.transpose(1, 2, 0).reshape(2, 2, -1, depth)

    which = lax.broadcasted_iota(jnp.int32, (2, share, depth), 0)
    near = shifted(jnp.where(which == 0, stream_a[None], stream_b[None]), "zh")
    near_a = in_order([v[0] for v in near], "zh").reshape(-1, depth)
    near_b = in_order([v[1] for v in near], "zh").reshape(-1, depth)
    near_b, near_a = together(near_b, "x", near_a, "y")
    near_b, near_a = in_order(near_b, "x", turn()), in_order(near_a, "y", turn())
    near_b, near_a = together(near_b, "y", near_a, "x")
    mine, other = project(near_a, near_b, up_a, up_b)
    near = swapped(other, "core")
    keep, give = mine[0] + near[0], mine[1] + near[1]
    act_b = (keep[0] + swapped(give[0], "zl")).astype(jnp.bfloat16)
    act_b, give_a = lax.optimization_barrier((act_b, give[1]))
    near, away_a = lax.optimization_barrier((shifted(act_b, "zh"), swapped(give_a, "zl")))
    act_a = (keep[1] + away_a).astype(jnp.bfloat16)

    first = in_order([v[:, :half] for v in near], "zh")
    second = in_order([v[:, half:] for v in near], "zh")
    first, second = together(first, "x", second, "y")
    first, second = in_order(first, "x", turn()), in_order(second, "y", turn())
    ours = crossed(act_a, COL)
    first, second = together(first, "y", second, "x")

    plan, row_mass = make_plan(first, second, ours, gumbel)
    for step in range(ITERS):
        if step > 0:
            row_mass = row_sums(plan, hid_sum(col_mass))
        row_mass = sum(crossed(row_mass, COL))
        col_mass = col_sums(plan, row_mass)
    return (-jnp.log(row_mass[0]), -jnp.log(hid_share(col_mass)))


def solution(mesh):
    fine = Mesh(mesh.devices.reshape(4, 4, 4, 2, 2), HID + COL)
    placed = (
        P(HID, COL),
        P(HID, COL),
        P(COL, HID),
        P(COL, None, HID),
        P(HID, COL),
    )
    return jax.shard_map(
        local, mesh=fine, in_specs=placed, out_specs=(P(HID), P(COL, HID)), check_vma=False
    )
```

```python
import jax
import jax.numpy as jnp
from jax import lax
from jax.experimental import pallas as pl
from jax.experimental.pallas import tpu as pltpu
from jax.sharding import Mesh, PartitionSpec as P

ITERS = 3


EPS = 1e-06
SHARPNESS = 32.0

HID = ("y", "zh", "x")
COL = ("zl", "core")
TILE = 256


def shifted(value, axis):
    size = lax.axis_size(axis)
    return [value] + [
        lax.ppermute(value, axis, [(i, (i + shift) % size) for i in range(size)])
        for shift in range(1, size)
    ]


def crossed(value, axes):
    size = lax.axis_size(axes)
    return [value] + [
        lax.ppermute(value, axes, [(i, i ^ flip) for i in range(size)]) for flip in range(1, size)
    ]


def pinned(values):
    return [pltpu.with_memory_space_constraint(value, pltpu.HBM) for value in values]


def across_chips(value, shift, early):
    pairs = []
    for y in range(4):
        for x in range(4):
            for core in range(2):
                if (core == 0) == early:
                    to = (4 * y + (x + shift) % 4) * 2 + core
                else:
                    to = (4 * ((y + shift) % 4) + x) * 2 + core
                pairs.append(((4 * y + x) * 2 + core, to))
    return lax.ppermute(value, ("y", "x", "core"), pairs)


def early_gather(value):
    value = lax.optimization_barrier(value)
    near = [value] + [across_chips(value, shift, True) for shift in (1, 2, 3)]
    near = lax.optimization_barrier(near)
    me = jnp.where(lax.axis_index("core") == 0, lax.axis_index("x"), lax.axis_index("y"))
    return placed(near, me)


def late_gather(value):
    value = lax.optimization_barrier(value)
    half = value.shape[0] // 2
    back = across_chips(value, 1, False)
    ahead = across_chips(value, 3, False)
    low = across_chips(back[:half], 1, False)
    high = across_chips(ahead[half:], 3, False)
    return lax.optimization_barrier([value, back, ahead, low, high])


LATE = ((0, 0, 4), (1, 0, 4), (3, 0, 4), (2, 0, 2), (2, 2, 2))


def hid_sum(value):
    for axis in ("x", "zh", "y"):
        value = sum(shifted(value, axis))
    return value


def hid_share(value):
    parts = value.reshape(lax.axis_size(HID), -1)
    return jnp.sum(lax.all_to_all(parts, HID, 0, 0, tiled=True), axis=0, keepdims=True)


def placed(near, me):
    size = len(near)
    return jnp.stack(
        [lax.select_n((me - spot + size) % size, *near) for spot in range(size)], axis=0
    )


def in_order(near, axis):
    return placed(near, lax.axis_index(axis))


def project_kernel(place, *refs):
    near = refs[0:5]
    up_a, up_b, mine, other, weights_a, weights_b, held_a, held_b, sem = refs[5:]
    y, x, zl, core = (place[i] for i in range(4))
    loads = [
        pltpu.make_async_copy(up_b, weights_b, sem.at[10]),
        pltpu.make_async_copy(up_a, weights_a, sem.at[11]),
    ]
    rows, cols = [], []
    for slot, held in enumerate((held_b, held_a)):
        for i, (back, start, size) in enumerate(LATE):
            at_y = lax.rem(y - back + 4, 4)
            at_x = lax.rem(x - back + 4, 4)
            source, spot = near[i].at[:, slot], pl.ds(start, size)
            signal = sem.at[5 * slot + i]
            rows.append(pltpu.make_async_copy(source, held.at[at_y, spot], signal))
            cols.append(pltpu.make_async_copy(source, held.at[spot, at_x], signal))
    for load in loads:
        load.start()

    @pl.when(core == 0)
    def _():
        for move in rows:
            move.start()

    @pl.when(core == 1)
    def _():
        for move in cols:
            move.start()

    depth = held_a.shape[-1]
    for slot, held, weights in ((0, held_b, weights_b), (1, held_a, weights_a)):
        loads[slot].wait()
        for move in rows[5 * slot : 5 * slot + 5]:
            move.wait()
        tokens = held[...].reshape(-1, depth)
        for out, which in ((other, 1 - core), (mine, core)):
            part = jnp.stack([weights[zl, which], weights[1 - zl, which]], axis=0)
            found = lax.dot_general(
                part.reshape(-1, depth),
                tokens,
                (((1,), (1,)), ((), ())),
                preferred_element_type=jnp.float32,
            )
            out[:, slot] = found.reshape(2, -1, found.shape[1])


def project(near, weights_a, weights_b):
    _, _, width, depth = weights_a.shape
    rows = near[0].shape[2]
    count = 16 * rows
    place = jnp.stack([lax.axis_index(axis) for axis in ("y", "x", "zl", "core")]).astype(jnp.int32)
    inside = pl.BlockSpec(memory_space=pltpu.VMEM)
    out = jax.ShapeDtypeStruct((2, 2, width, count), jnp.float32)
    return pl.pallas_call(
        project_kernel,
        in_specs=[pl.BlockSpec(memory_space=pltpu.SMEM)]
        + [pl.BlockSpec(memory_space=pl.ANY)] * 5
        + [pl.BlockSpec(memory_space=pltpu.HBM)] * 2,
        out_specs=[inside, inside],
        scratch_shapes=[
            pltpu.VMEM(weights_a.shape, jnp.bfloat16),
            pltpu.VMEM(weights_b.shape, jnp.bfloat16),
            pltpu.VMEM((4, 4, rows, depth), jnp.bfloat16),
            pltpu.VMEM((4, 4, rows, depth), jnp.bfloat16),
            pltpu.SemaphoreType.DMA((12,)),
        ],
        out_shape=[out, out],
        compiler_params=pltpu.CompilerParams(vmem_limit_bytes=20 * 1024 * 1024),
        cost_estimate=pl.CostEstimate(
            flops=2 * 8 * width * depth * count,
            bytes_accessed=(8 * width + 2 * count) * depth * 2,
            transcendentals=0,
        ),
    )(place, *near, *pinned([weights_a, weights_b]))


def swapped(value, axis):
    return lax.ppermute(value, axis, [(0, 1), (1, 0)])


def padded(rows):
    return -(-rows // 128) * 128


def across(total):
    return jnp.sum(total[...].T, axis=0, keepdims=True)


def row_kernel(plan, col_mass, mass, scale, total):
    rows, columns = plan.shape
    scale[...] = 1.0 / col_mass[...]
    total[...] = jnp.zeros_like(total)

    def body(block, carry):
        spot = pl.ds(pl.multiple_of(block * 64, 64), 64)
        found = jnp.zeros((64, 128), jnp.float32)
        for lane in range(0, columns, 128):
            found = found + plan[spot, lane : lane + 128] * scale[:, lane : lane + 128]
        total[spot, :] = found
        return carry

    lax.fori_loop(0, rows // 64, body, 0)
    mass[...] = across(total)[:, :rows]


def col_kernel(plan, row_mass, mass, scale, wide):
    rows, columns = plan.shape
    scale[...] = jnp.ones_like(scale)
    scale[:, :rows] = 1.0 / row_mass[...]
    wide[...] = jnp.broadcast_to(scale[...], (128, scale.shape[1])).T

    def body(block, carry):
        spot = pl.ds(pl.multiple_of(block * 1024, 1024), 1024)
        found = jnp.zeros((8, 1024), jnp.float32)
        for row in range(0, rows, 8):
            factor = jnp.concatenate([wide[row : row + 8, :]] * 8, axis=1)
            found = found + plan[row : row + 8, spot] * factor
        mass[:, spot] = jnp.sum(found, axis=0, keepdims=True)
        return carry

    lax.fori_loop(0, columns // 1024, body, 0)


def plan_pass(kernel, plan, mass, width, scratch):
    inside = pl.BlockSpec(memory_space=pltpu.VMEM)
    return pl.pallas_call(
        kernel,
        in_specs=[inside, inside],
        out_specs=inside,
        out_shape=jax.ShapeDtypeStruct((1, width), jnp.float32),
        scratch_shapes=[pltpu.VMEM(shape, jnp.float32) for shape in scratch],
        compiler_params=pltpu.CompilerParams(vmem_limit_bytes=4 * 1024 * 1024),
        cost_estimate=pl.CostEstimate(
            flops=2 * plan.size, bytes_accessed=4 * plan.size, transcendentals=0
        ),
    )(pltpu.with_memory_space_constraint(plan, pltpu.VMEM), mass)


def row_sums(plan, col_mass):
    rows, columns = plan.shape
    return plan_pass(row_kernel, plan, col_mass, rows, [(1, columns), (padded(rows), 128)])


def col_sums(plan, row_mass):
    rows, columns = plan.shape
    return plan_pass(
        col_kernel, plan, row_mass, columns, [(1, padded(rows)), (padded(rows), 128)]
    )


def plan_kernel(place, *refs):
    near, ours = refs[0:5], refs[5:9]
    noise, plan, mass, held_b, held_a, gumbel, inv_a, total, sem_b, sem_a, sem_g = refs[9:]
    step = pl.program_id(0)
    rows, columns = plan.shape
    width = columns // 4
    y, x, c, core = (place[i] for i in range(4))

    def noise_move(block):
        spot = pl.ds(pl.multiple_of(block * width, width), width)
        return pltpu.make_async_copy(noise.at[:, spot], gumbel.at[block], sem_g.at[block])

    @pl.when(step == 0)
    def _():
        moves = [
            pltpu.make_async_copy(ours[flip], held_a.at[c ^ flip], sem_a.at[flip])
            for flip in range(4)
        ]
        by_row, by_col = [], []
        for i, (back, start, size) in enumerate(LATE):
            at_y = lax.rem(y - back + 4, 4)
            at_x = lax.rem(x - back + 4, 4)
            for spot in range(size):
                source, signal = near[i].at[spot], sem_b.at[len(by_row)]
                by_row.append(
                    pltpu.make_async_copy(source, held_b.at[at_y, :, start + spot], signal)
                )
                by_col.append(
                    pltpu.make_async_copy(source, held_b.at[start + spot, :, at_x], signal)
                )
        for move in moves:
            move.start()
        noise_move(0).start()

        @pl.when(core == 0)
        def _():
            for move in by_row:
                move.start()

        @pl.when(core == 1)
        def _():
            for move in by_col:
                move.start()

        for block in range(1, 4):
            noise_move(block).start()
        for move in moves:
            move.wait()
        values = held_a[...].reshape(rows, -1).astype(jnp.float32)
        scale = SHARPNESS / values.shape[1]
        inv_a[...] = scale * lax.rsqrt(jnp.mean(values * values, axis=1, keepdims=True) + EPS)
        total[...] = jnp.zeros_like(total)
        for move in by_row:
            move.wait()

    noise_move(step).wait()
    left = held_a[...].reshape(rows, -1)
    flat = held_b.reshape(4 * width, left.shape[1])
    for tile in range(width // TILE):
        right = flat[pl.ds(pl.multiple_of(step * width + tile * TILE, TILE), TILE), :]
        cross = lax.dot_general(
            left, right, (((1,), (1,)), ((), ())), preferred_element_type=jnp.float32
        )
        square = right.astype(jnp.float32)
        square = square * square
        folded = square[:, :128]
        for lane in range(128, square.shape[1], 128):
            folded = folded + square[:, lane : lane + 128]
        power = jnp.sum(folded.T, axis=0, keepdims=True)
        inv_b = lax.rsqrt(power / square.shape[1] + EPS)
        spot = pl.ds(tile * TILE, TILE)
        noisy = gumbel[step, :, spot].astype(jnp.float32)
        value = jnp.exp(cross * inv_a[...] * inv_b + noisy)
        plan[:, pl.ds(pl.multiple_of(step * width + tile * TILE, TILE), TILE)] = value
        total[:rows, :] += value[:, :128] + value[:, 128:]

    @pl.when(step == pl.num_programs(0) - 1)
    def _():
        mass[...] = across(total)[:, :rows]


def make_plan(near, ours, gumbel):
    rows, columns = gumbel.shape
    share, count = ours[0].shape
    width = columns // 4
    place = jnp.stack(
        [lax.axis_index("y"), lax.axis_index("x"), lax.axis_index(COL), lax.axis_index("core")]
    ).astype(jnp.int32)
    return pl.pallas_call(
        plan_kernel,
        grid_spec=pltpu.PrefetchScalarGridSpec(
            num_scalar_prefetch=1,
            grid=(4,),
            in_specs=[pl.BlockSpec(memory_space=pl.ANY)] * 9
            + [pl.BlockSpec(memory_space=pltpu.HBM)],
            out_specs=[
                pl.BlockSpec(memory_space=pltpu.VMEM),
                pl.BlockSpec((1, rows), lambda i, p: (0, 0)),
            ],
            scratch_shapes=[
                pltpu.VMEM((4, 4, 4, share, count), jnp.bfloat16),
                pltpu.VMEM((4, share, count), jnp.bfloat16),
                pltpu.VMEM((4, rows, width), jnp.bfloat16),
                pltpu.VMEM((rows, 1), jnp.float32),
                pltpu.VMEM((padded(rows), 128), jnp.float32),
                pltpu.SemaphoreType.DMA((16,)),
                pltpu.SemaphoreType.DMA((4,)),
                pltpu.SemaphoreType.DMA((4,)),
            ],
        ),
        out_shape=[
            pltpu.VMEM((rows, columns), jnp.float32),
            jax.ShapeDtypeStruct((1, rows), jnp.float32),
        ],
        compiler_params=pltpu.CompilerParams(
            dimension_semantics=("arbitrary",), vmem_limit_bytes=26 * 1024 * 1024
        ),
        cost_estimate=pl.CostEstimate(
            flops=2 * rows * columns * count,
            bytes_accessed=rows * columns * 6 + columns * count * 2,
            transcendentals=rows * columns,
        ),
    )(place, *near, *ours, *pinned([gumbel]))


def local(stream_a, stream_b, up_a, up_b, gumbel):
    share, depth = stream_a.shape
    up_a = up_a.T.reshape(2, 2, -1, depth)
    up_b = up_b.transpose(1, 2, 0).reshape(2, 2, -1, depth)

    which = lax.broadcasted_iota(jnp.int32, (2, share, depth), 0)
    near = shifted(jnp.where(which == 0, stream_b[None], stream_a[None]), "zh")
    near = [in_order([v[i] for v in near], "zh").reshape(-1, depth) for i in range(2)]
    near = late_gather(early_gather(jnp.stack(near, axis=0)))
    mine, other = project(near, up_a, up_b)
    near = swapped(other, "core")
    keep, give = mine[0] + near[0], mine[1] + near[1]
    act_b = (keep[0] + swapped(give[0], "zl")).astype(jnp.bfloat16)
    act_b, give_a = lax.optimization_barrier((act_b, give[1]))
    near, away_a = lax.optimization_barrier((shifted(act_b, "zh"), swapped(give_a, "zl")))
    act_a = (keep[1] + away_a).astype(jnp.bfloat16)

    near = early_gather(in_order(near, "zh"))
    ours = crossed(act_a, COL)
    near = late_gather(near)

    plan, row_mass = make_plan(near, ours, gumbel)
    for step in range(ITERS):
        if step > 0:
            row_mass = row_sums(plan, hid_sum(col_mass))
        row_mass = sum(crossed(row_mass, COL))
        col_mass = col_sums(plan, row_mass)
    return (-jnp.log(row_mass[0]), -jnp.log(hid_share(col_mass)))


def solution(mesh):
    fine = Mesh(mesh.devices.reshape(4, 4, 4, 2, 2), HID + COL)
    placed = (
        P(HID, COL),
        P(HID, COL),
        P(COL, HID),
        P(COL, None, HID),
        P(HID, COL),
    )
    return jax.shard_map(
        local, mesh=fine, in_specs=placed, out_specs=(P(HID), P(COL, HID)), check_vma=False
    )
```

```python
import jax
import jax.numpy as jnp
from jax import lax
from jax.experimental import pallas as pl
from jax.experimental.pallas import tpu as pltpu
from jax.sharding import Mesh, PartitionSpec as P

ITERS = 3


EPS = 1e-06
SHARPNESS = 32.0

HID = ("y", "zh", "x")
COL = ("zl", "core")
TILE = 256


def shifted(value, axis):
    size = lax.axis_size(axis)
    return [value] + [
        lax.ppermute(value, axis, [(i, (i + shift) % size) for i in range(size)])
        for shift in range(1, size)
    ]


def crossed(value, axes):
    size = lax.axis_size(axes)
    return [value] + [
        lax.ppermute(value, axes, [(i, i ^ flip) for i in range(size)]) for flip in range(1, size)
    ]


def pinned(values, space=pltpu.HBM):
    return [pltpu.with_memory_space_constraint(value, space) for value in values]


def across_chips(value, shift, early):
    pairs = []
    for y in range(4):
        for x in range(4):
            for core in range(2):
                if (core == 0) == early:
                    to = (4 * y + (x + shift) % 4) * 2 + core
                else:
                    to = (4 * ((y + shift) % 4) + x) * 2 + core
                pairs.append(((4 * y + x) * 2 + core, to))
    return lax.ppermute(value, ("y", "x", "core"), pairs)


def early_gather(value, give=None):
    value, give = lax.optimization_barrier((value, give))
    near = [value] + [across_chips(value, shift, True) for shift in (1, 2, 3)]
    got = None if give is None else swapped(give, "zl")
    near, got = lax.optimization_barrier((near, got))
    me = jnp.where(lax.axis_index("core") == 0, lax.axis_index("x"), lax.axis_index("y"))
    return placed(near, me), got


def late_gather(value):
    value = lax.optimization_barrier(value)
    half = value.shape[0] // 2
    back = across_chips(value, 1, False)
    ahead = across_chips(value, 3, False)
    low = across_chips(back[:half], 1, False)
    high = across_chips(ahead[half:], 3, False)
    return lax.optimization_barrier([value, back, ahead, low, high])


LATE = ((0, 0, 4), (1, 0, 4), (3, 0, 4), (2, 0, 2), (2, 2, 2))


def hid_sum(value):
    for axis in ("x", "zh", "y"):
        value = sum(shifted(value, axis))
    return value


def hid_share(value):
    parts = value.reshape(lax.axis_size(HID), -1)
    return jnp.sum(lax.all_to_all(parts, HID, 0, 0, tiled=True), axis=0, keepdims=True)


def placed(near, me):
    size = len(near)
    return jnp.stack(
        [lax.select_n((me - spot + size) % size, *near) for spot in range(size)], axis=0
    )


def in_order(near, axis):
    return placed(near, lax.axis_index(axis))


def project_kernel(place, *refs):
    near = refs[0:5]
    up_a, up_b, mine, other, weights_a, weights_b, held_a, held_b, sem = refs[5:]
    y, x, zl, core = (place[i] for i in range(4))
    loads = [
        pltpu.make_async_copy(up_b, weights_b, sem.at[10]),
        pltpu.make_async_copy(up_a, weights_a, sem.at[11]),
    ]
    rows, cols = [], []
    for slot, held in enumerate((held_b, held_a)):
        for i, (back, start, size) in enumerate(LATE):
            at_y = lax.rem(y - back + 4, 4)
            at_x = lax.rem(x - back + 4, 4)
            source, spot = near[i].at[:, slot], pl.ds(start, size)
            signal = sem.at[5 * slot + i]
            rows.append(pltpu.make_async_copy(source, held.at[at_y, spot], signal))
            cols.append(pltpu.make_async_copy(source, held.at[spot, at_x], signal))
    for load in loads:
        load.start()

    @pl.when(core == 0)
    def _():
        for move in rows:
            move.start()

    @pl.when(core == 1)
    def _():
        for move in cols:
            move.start()

    depth = held_a.shape[-1]
    for slot, held, weights in ((0, held_b, weights_b), (1, held_a, weights_a)):
        loads[slot].wait()
        for move in rows[5 * slot : 5 * slot + 5]:
            move.wait()
        tokens = held[...].reshape(-1, depth)
        for out, which in ((other, 1 - core), (mine, core)):
            part = jnp.stack([weights[zl, which], weights[1 - zl, which]], axis=0)
            found = lax.dot_general(
                part.reshape(-1, depth),
                tokens,
                (((1,), (1,)), ((), ())),
                preferred_element_type=jnp.float32,
            )
            out[:, slot] = found.reshape(2, -1, found.shape[1])


def project(near, weights_a, weights_b):
    _, _, width, depth = weights_a.shape
    rows = near[0].shape[2]
    count = 16 * rows
    place = jnp.stack([lax.axis_index(axis) for axis in ("y", "x", "zl", "core")]).astype(jnp.int32)
    inside = pl.BlockSpec(memory_space=pltpu.VMEM)
    out = jax.ShapeDtypeStruct((2, 2, width, count), jnp.float32)
    return pl.pallas_call(
        project_kernel,
        in_specs=[pl.BlockSpec(memory_space=pltpu.SMEM)]
        + [pl.BlockSpec(memory_space=pl.ANY)] * 5
        + [pl.BlockSpec(memory_space=pltpu.HBM)] * 2,
        out_specs=[inside, inside],
        scratch_shapes=[
            pltpu.VMEM(weights_a.shape, jnp.bfloat16),
            pltpu.VMEM(weights_b.shape, jnp.bfloat16),
            pltpu.VMEM((4, 4, rows, depth), jnp.bfloat16),
            pltpu.VMEM((4, 4, rows, depth), jnp.bfloat16),
            pltpu.SemaphoreType.DMA((12,)),
        ],
        out_shape=[out, out],
        compiler_params=pltpu.CompilerParams(vmem_limit_bytes=20 * 1024 * 1024),
        cost_estimate=pl.CostEstimate(
            flops=2 * 8 * width * depth * count,
            bytes_accessed=(8 * width + 2 * count) * depth * 2,
            transcendentals=0,
        ),
    )(place, *near, *pinned([weights_a, weights_b]))


def swapped(value, axis):
    return lax.ppermute(value, axis, [(0, 1), (1, 0)])


def padded(rows):
    return -(-rows // 128) * 128


def across(total):
    return jnp.sum(total[...].T, axis=0, keepdims=True)


def row_kernel(plan, col_mass, mass, scale, total):
    rows, columns = plan.shape
    scale[...] = 1.0 / col_mass[...]
    total[...] = jnp.zeros_like(total)

    def body(block, carry):
        spot = pl.ds(pl.multiple_of(block * 64, 64), 64)
        found = jnp.zeros((64, 128), jnp.float32)
        for lane in range(0, columns, 128):
            found = found + plan[spot, lane : lane + 128] * scale[:, lane : lane + 128]
        total[spot, :] = found
        return carry

    lax.fori_loop(0, rows // 64, body, 0)
    mass[...] = across(total)[:, :rows]


def col_kernel(plan, row_mass, mass, scale, wide):
    rows, columns = plan.shape
    scale[...] = jnp.ones_like(scale)
    scale[:, :rows] = 1.0 / row_mass[...]
    wide[...] = jnp.broadcast_to(scale[...], (128, scale.shape[1])).T

    def body(block, carry):
        spot = pl.ds(pl.multiple_of(block * 1024, 1024), 1024)
        found = jnp.zeros((8, 1024), jnp.float32)
        for row in range(0, rows, 8):
            factor = jnp.concatenate([wide[row : row + 8, :]] * 8, axis=1)
            found = found + plan[row : row + 8, spot] * factor
        mass[:, spot] = jnp.sum(found, axis=0, keepdims=True)
        return carry

    lax.fori_loop(0, columns // 1024, body, 0)


def plan_pass(kernel, plan, mass, width, scratch):
    inside = pl.BlockSpec(memory_space=pltpu.VMEM)
    return pl.pallas_call(
        kernel,
        in_specs=[inside, inside],
        out_specs=inside,
        out_shape=jax.ShapeDtypeStruct((1, width), jnp.float32),
        scratch_shapes=[pltpu.VMEM(shape, jnp.float32) for shape in scratch],
        compiler_params=pltpu.CompilerParams(vmem_limit_bytes=4 * 1024 * 1024),
        cost_estimate=pl.CostEstimate(
            flops=2 * plan.size, bytes_accessed=4 * plan.size, transcendentals=0
        ),
    )(pltpu.with_memory_space_constraint(plan, pltpu.VMEM), mass)


def row_sums(plan, col_mass):
    rows, columns = plan.shape
    return plan_pass(row_kernel, plan, col_mass, rows, [(1, columns), (padded(rows), 128)])


def col_sums(plan, row_mass):
    rows, columns = plan.shape
    return plan_pass(
        col_kernel, plan, row_mass, columns, [(1, padded(rows)), (padded(rows), 128)]
    )


def plan_kernel(place, *refs):
    near, ours = refs[0:5], refs[5:9]
    noise, plan, mass, held_b, held_a, gumbel, inv_a, total, sem_b, sem_a, sem_g = refs[9:]
    step = pl.program_id(0)
    rows, columns = plan.shape
    width = columns // 4
    y, x, c, core = (place[i] for i in range(4))

    def noise_move(block):
        spot = pl.ds(pl.multiple_of(block * width, width), width)
        return pltpu.make_async_copy(noise.at[:, spot], gumbel.at[block], sem_g.at[block])

    def block_move(source, at_y, at_x):
        return pltpu.make_async_copy(source, held_b.at[at_y, :, at_x], sem_b.at[at_y, at_x])

    @pl.when(step == 0)
    def _():
        moves = [
            pltpu.make_async_copy(ours[flip], held_a.at[c ^ flip], sem_a.at[flip])
            for flip in range(4)
        ]
        by_row, by_col = [], []
        for i, (back, start, size) in enumerate(LATE):
            at_y = lax.rem(y - back + 4, 4)
            at_x = lax.rem(x - back + 4, 4)
            for spot in range(size):
                line = start + spot
                by_row.append(block_move(near[i].at[spot], at_y, line))
                by_col.append((line, block_move(near[i].at[spot], line, at_x)))
        for move in moves:
            move.start()
        noise_move(0).start()

        @pl.when(core == 0)
        def _():
            for move in by_row:
                move.start()

        @pl.when(core == 1)
        def _():
            for _, move in sorted(by_col, key=lambda pair: pair[0]):
                move.start()

        for block in range(1, 4):
            noise_move(block).start()
        for move in moves:
            move.wait()
        values = held_a[...].reshape(rows, -1).astype(jnp.float32)
        scale = SHARPNESS / values.shape[1]
        inv_a[...] = scale * lax.rsqrt(jnp.mean(values * values, axis=1, keepdims=True) + EPS)
        total[...] = jnp.zeros_like(total)

    for line in range(4):
        block_move(near[0].at[0], step, line).wait()
    noise_move(step).wait()
    left = held_a[...].reshape(rows, -1)
    flat = held_b.reshape(4 * width, left.shape[1])
    for tile in range(width // TILE):
        right = flat[pl.ds(pl.multiple_of(step * width + tile * TILE, TILE), TILE), :]
        cross = lax.dot_general(
            left, right, (((1,), (1,)), ((), ())), preferred_element_type=jnp.float32
        )
        square = right.astype(jnp.float32)
        square = square * square
        folded = square[:, :128]
        for lane in range(128, square.shape[1], 128):
            folded = folded + square[:, lane : lane + 128]
        power = jnp.sum(folded.T, axis=0, keepdims=True)
        inv_b = lax.rsqrt(power / square.shape[1] + EPS)
        spot = pl.ds(tile * TILE, TILE)
        noisy = gumbel[step, :, spot].astype(jnp.float32)
        value = jnp.exp(cross * inv_a[...] * inv_b + noisy)
        plan[:, pl.ds(pl.multiple_of(step * width + tile * TILE, TILE), TILE)] = value
        total[:rows, :] += value[:, :128] + value[:, 128:]

    @pl.when(step == pl.num_programs(0) - 1)
    def _():
        mass[...] = across(total)[:, :rows]


def make_plan(near, ours, gumbel):
    rows, columns = gumbel.shape
    share, count = ours[0].shape
    width = columns // 4
    place = jnp.stack(
        [lax.axis_index("y"), lax.axis_index("x"), lax.axis_index(COL), lax.axis_index("core")]
    ).astype(jnp.int32)
    return pl.pallas_call(
        plan_kernel,
        grid_spec=pltpu.PrefetchScalarGridSpec(
            num_scalar_prefetch=1,
            grid=(4,),
            in_specs=[pl.BlockSpec(memory_space=pl.ANY)] * 9
            + [pl.BlockSpec(memory_space=pltpu.HBM)],
            out_specs=[
                pl.BlockSpec(memory_space=pltpu.VMEM),
                pl.BlockSpec((1, rows), lambda i, p: (0, 0)),
            ],
            scratch_shapes=[
                pltpu.VMEM((4, 4, 4, share, count), jnp.bfloat16),
                pltpu.VMEM((4, share, count), jnp.bfloat16),
                pltpu.VMEM((4, rows, width), jnp.bfloat16),
                pltpu.VMEM((rows, 1), jnp.float32),
                pltpu.VMEM((padded(rows), 128), jnp.float32),
                pltpu.SemaphoreType.DMA((4, 4)),
                pltpu.SemaphoreType.DMA((4,)),
                pltpu.SemaphoreType.DMA((4,)),
            ],
        ),
        out_shape=[
            pltpu.VMEM((rows, columns), jnp.float32),
            jax.ShapeDtypeStruct((1, rows), jnp.float32),
        ],
        compiler_params=pltpu.CompilerParams(
            dimension_semantics=("arbitrary",), vmem_limit_bytes=26 * 1024 * 1024
        ),
        cost_estimate=pl.CostEstimate(
            flops=2 * rows * columns * count,
            bytes_accessed=rows * columns * 6 + columns * count * 2,
            transcendentals=rows * columns,
        ),
    )(place, *pinned(near, pltpu.VMEM), *ours, *pinned([gumbel]))


def local(stream_a, stream_b, up_a, up_b, gumbel):
    share, depth = stream_a.shape
    up_a = up_a.T.reshape(2, 2, -1, depth)
    up_b = up_b.transpose(1, 2, 0).reshape(2, 2, -1, depth)

    which = lax.broadcasted_iota(jnp.int32, (2, share, depth), 0)
    near = shifted(jnp.where(which == 0, stream_b[None], stream_a[None]), "zh")
    near = [in_order([v[i] for v in near], "zh").reshape(-1, depth) for i in range(2)]
    near = late_gather(early_gather(jnp.stack(near, axis=0))[0])
    mine, other = project(near, up_a, up_b)
    near = swapped(other, "core")
    keep, give = mine[0] + near[0], mine[1] + near[1]
    act_b = (keep[0] + swapped(give[0], "zl")).astype(jnp.bfloat16)
    near = in_order(shifted(act_b, "zh"), "zh")
    near, away_a = early_gather(near, give[1])
    act_a = (keep[1] + away_a).astype(jnp.bfloat16)
    ours = crossed(act_a, COL)
    near = late_gather(near)

    plan, row_mass = make_plan(near, ours, gumbel)
    for step in range(ITERS):
        if step > 0:
            row_mass = row_sums(plan, hid_sum(col_mass))
        row_mass = sum(crossed(row_mass, COL))
        col_mass = col_sums(plan, row_mass)
    return (-jnp.log(row_mass[0]), -jnp.log(hid_share(col_mass)))


def solution(mesh):
    fine = Mesh(mesh.devices.reshape(4, 4, 4, 2, 2), HID + COL)
    placed = (
        P(HID, COL),
        P(HID, COL),
        P(COL, HID),
        P(COL, None, HID),
        P(HID, COL),
    )
    return jax.shard_map(
        local, mesh=fine, in_specs=placed, out_specs=(P(HID), P(COL, HID)), check_vma=False
    )
```

```python
import jax
import jax.numpy as jnp
from jax import lax
from jax.experimental import pallas as pl
from jax.experimental.pallas import tpu as pltpu
from jax.sharding import Mesh, PartitionSpec as P

ITERS = 3


EPS = 1e-06
SHARPNESS = 32.0

HID = ("y", "zh", "x")
COL = ("zl", "core")
TILE = 256


def shifted(value, axis):
    size = lax.axis_size(axis)
    return [value] + [
        lax.ppermute(value, axis, [(i, (i + shift) % size) for i in range(size)])
        for shift in range(1, size)
    ]


def crossed(value, axes):
    size = lax.axis_size(axes)
    return [value] + [
        lax.ppermute(value, axes, [(i, i ^ flip) for i in range(size)]) for flip in range(1, size)
    ]


def pinned(values, space=pltpu.HBM):
    return [pltpu.with_memory_space_constraint(value, space) for value in values]


def across_chips(value, shift, early):
    pairs = []
    for y in range(4):
        for x in range(4):
            for core in range(2):
                if (core == 0) == early:
                    to = (4 * y + (x + shift) % 4) * 2 + core
                else:
                    to = (4 * ((y + shift) % 4) + x) * 2 + core
                pairs.append(((4 * y + x) * 2 + core, to))
    return lax.ppermute(value, ("y", "x", "core"), pairs)


def early_gather(value, give=None):
    value, give = lax.optimization_barrier((value, give))
    near = [value] + [across_chips(value, shift, True) for shift in (1, 2, 3)]
    got = None if give is None else swapped(give, "zl")
    near = lax.optimization_barrier(near)
    me = jnp.where(lax.axis_index("core") == 0, lax.axis_index("x"), lax.axis_index("y"))
    return (placed(near, me, (0, 1)), placed(near, me, (2, 3))), got


def late_gather(halves):
    low, high = lax.optimization_barrier(halves)
    low_back = across_chips(low, 1, False)
    high_ahead = across_chips(high, 3, False)
    high_back = across_chips(high, 1, False)
    low_ahead = across_chips(low, 3, False)
    low_away = across_chips(low_back, 1, False)
    high_away = across_chips(high_ahead, 3, False)
    return lax.optimization_barrier(
        [low, high, low_back, high_back, low_away, high_away, low_ahead, high_ahead]
    )


def hid_sum(value):
    for axis in ("x", "zh", "y"):
        value = sum(shifted(value, axis))
    return value


def hid_share(value):
    parts = value.reshape(lax.axis_size(HID), -1)
    return jnp.sum(lax.all_to_all(parts, HID, 0, 0, tiled=True), axis=0, keepdims=True)


def placed(near, me, spots):
    size = len(near)
    return jnp.stack(
        [lax.select_n((me - spot + size) % size, *near) for spot in spots], axis=0
    )


def in_order(near, axis):
    return placed(near, lax.axis_index(axis), range(len(near)))


def project_kernel(place, *refs):
    near = refs[0:8]
    up_a, up_b, mine, other, weights_a, weights_b, held_a, held_b, sem = refs[8:]
    y, x, zl, core = (place[i] for i in range(4))
    loads = [
        pltpu.make_async_copy(up_b, weights_b, sem.at[16]),
        pltpu.make_async_copy(up_a, weights_a, sem.at[17]),
    ]
    rows, cols = [], []
    for slot, held in enumerate((held_b, held_a)):
        for i in range(8):
            at_y = lax.rem(y - i // 2 + 4, 4)
            at_x = lax.rem(x - i // 2 + 4, 4)
            source, spot = near[i].at[:, slot], pl.ds(2 * (i % 2), 2)
            signal = sem.at[8 * slot + i]
            rows.append(pltpu.make_async_copy(source, held.at[at_y, spot], signal))
            cols.append(pltpu.make_async_copy(source, held.at[spot, at_x], signal))
    for load in loads:
        load.start()

    @pl.when(core == 0)
    def _():
        for move in rows:
            move.start()

    @pl.when(core == 1)
    def _():
        for move in cols:
            move.start()

    depth = held_a.shape[-1]
    for slot, held, weights in ((0, held_b, weights_b), (1, held_a, weights_a)):
        loads[slot].wait()
        for move in rows[8 * slot : 8 * slot + 8]:
            move.wait()
        tokens = held[...].reshape(-1, depth)
        for out, which in ((other, 1 - core), (mine, core)):
            part = jnp.stack([weights[zl, which], weights[1 - zl, which]], axis=0)
            found = lax.dot_general(
                part.reshape(-1, depth),
                tokens,
                (((1,), (1,)), ((), ())),
                preferred_element_type=jnp.float32,
            )
            out[:, slot] = found.reshape(2, -1, found.shape[1])


def project(near, weights_a, weights_b):
    _, _, width, depth = weights_a.shape
    rows = near[0].shape[2]
    count = 16 * rows
    place = jnp.stack([lax.axis_index(axis) for axis in ("y", "x", "zl", "core")]).astype(jnp.int32)
    inside = pl.BlockSpec(memory_space=pltpu.VMEM)
    out = jax.ShapeDtypeStruct((2, 2, width, count), jnp.float32)
    return pl.pallas_call(
        project_kernel,
        in_specs=[pl.BlockSpec(memory_space=pltpu.SMEM)]
        + [pl.BlockSpec(memory_space=pl.ANY)] * 8
        + [pl.BlockSpec(memory_space=pltpu.HBM)] * 2,
        out_specs=[inside, inside],
        scratch_shapes=[
            pltpu.VMEM(weights_a.shape, jnp.bfloat16),
            pltpu.VMEM(weights_b.shape, jnp.bfloat16),
            pltpu.VMEM((4, 4, rows, depth), jnp.bfloat16),
            pltpu.VMEM((4, 4, rows, depth), jnp.bfloat16),
            pltpu.SemaphoreType.DMA((18,)),
        ],
        out_shape=[out, out],
        compiler_params=pltpu.CompilerParams(vmem_limit_bytes=20 * 1024 * 1024),
        cost_estimate=pl.CostEstimate(
            flops=2 * 8 * width * depth * count,
            bytes_accessed=(8 * width + 2 * count) * depth * 2,
            transcendentals=0,
        ),
    )(place, *near, *pinned([weights_a, weights_b]))


def swapped(value, axis):
    return lax.ppermute(value, axis, [(0, 1), (1, 0)])


def padded(rows):
    return -(-rows // 128) * 128


def across(total):
    return jnp.sum(total[...].T, axis=0, keepdims=True)


def row_kernel(plan, col_mass, mass, scale, total):
    rows, columns = plan.shape
    scale[...] = 1.0 / col_mass[...]
    total[...] = jnp.zeros_like(total)

    def body(block, carry):
        spot = pl.ds(pl.multiple_of(block * 64, 64), 64)
        found = jnp.zeros((64, 128), jnp.float32)
        for lane in range(0, columns, 128):
            found = found + plan[spot, lane : lane + 128] * scale[:, lane : lane + 128]
        total[spot, :] = found
        return carry

    lax.fori_loop(0, rows // 64, body, 0)
    mass[...] = across(total)[:, :rows]


def col_kernel(plan, row_mass, mass, scale, wide):
    rows, columns = plan.shape
    scale[...] = jnp.ones_like(scale)
    scale[:, :rows] = 1.0 / row_mass[...]
    wide[...] = jnp.broadcast_to(scale[...], (128, scale.shape[1])).T

    def body(block, carry):
        spot = pl.ds(pl.multiple_of(block * 1024, 1024), 1024)
        found = jnp.zeros((8, 1024), jnp.float32)
        for row in range(0, rows, 8):
            factor = jnp.concatenate([wide[row : row + 8, :]] * 8, axis=1)
            found = found + plan[row : row + 8, spot] * factor
        mass[:, spot] = jnp.sum(found, axis=0, keepdims=True)
        return carry

    lax.fori_loop(0, columns // 1024, body, 0)


def plan_pass(kernel, plan, mass, width, scratch):
    inside = pl.BlockSpec(memory_space=pltpu.VMEM)
    return pl.pallas_call(
        kernel,
        in_specs=[inside, inside],
        out_specs=inside,
        out_shape=jax.ShapeDtypeStruct((1, width), jnp.float32),
        scratch_shapes=[pltpu.VMEM(shape, jnp.float32) for shape in scratch],
        compiler_params=pltpu.CompilerParams(vmem_limit_bytes=4 * 1024 * 1024),
        cost_estimate=pl.CostEstimate(
            flops=2 * plan.size, bytes_accessed=4 * plan.size, transcendentals=0
        ),
    )(pltpu.with_memory_space_constraint(plan, pltpu.VMEM), mass)


def row_sums(plan, col_mass):
    rows, columns = plan.shape
    return plan_pass(row_kernel, plan, col_mass, rows, [(1, columns), (padded(rows), 128)])


def col_sums(plan, row_mass):
    rows, columns = plan.shape
    return plan_pass(
        col_kernel, plan, row_mass, columns, [(1, padded(rows)), (padded(rows), 128)]
    )


def plan_kernel(place, *refs):
    near, ours = refs[0:8], refs[8:12]
    noise, plan, mass, held_b, held_a, gumbel, inv_a, total, sem_b, sem_a, sem_g = refs[12:]
    step = pl.program_id(0)
    rows, columns = plan.shape
    width = columns // 4
    y, x, c, core = (place[i] for i in range(4))

    def noise_move(block):
        spot = pl.ds(pl.multiple_of(block * width, width), width)
        return pltpu.make_async_copy(noise.at[:, spot], gumbel.at[block], sem_g.at[block])

    def block_move(source, at_y, at_x):
        return pltpu.make_async_copy(source, held_b.at[at_y, :, at_x], sem_b.at[at_y, at_x])

    @pl.when(step == 0)
    def _():
        moves = [
            pltpu.make_async_copy(ours[flip], held_a.at[c ^ flip], sem_a.at[flip])
            for flip in range(4)
        ]
        by_row, by_col = [], []
        for i in range(8):
            at_y = lax.rem(y - i // 2 + 4, 4)
            at_x = lax.rem(x - i // 2 + 4, 4)
            for spot in range(2):
                line = 2 * (i % 2) + spot
                by_row.append(block_move(near[i].at[spot], at_y, line))
                by_col.append((line, block_move(near[i].at[spot], line, at_x)))
        for move in moves:
            move.start()
        noise_move(0).start()

        @pl.when(core == 0)
        def _():
            for move in by_row:
                move.start()

        @pl.when(core == 1)
        def _():
            for _, move in sorted(by_col, key=lambda pair: pair[0]):
                move.start()

        for block in range(1, 4):
            noise_move(block).start()
        for move in moves:
            move.wait()
        values = held_a[...].reshape(rows, -1).astype(jnp.float32)
        scale = SHARPNESS / values.shape[1]
        inv_a[...] = scale * lax.rsqrt(jnp.mean(values * values, axis=1, keepdims=True) + EPS)
        total[...] = jnp.zeros_like(total)

    for line in range(4):
        block_move(near[0].at[0], step, line).wait()
    noise_move(step).wait()
    left = held_a[...].reshape(rows, -1)
    flat = held_b.reshape(4 * width, left.shape[1])
    for tile in range(width // TILE):
        right = flat[pl.ds(pl.multiple_of(step * width + tile * TILE, TILE), TILE), :]
        cross = lax.dot_general(
            left, right, (((1,), (1,)), ((), ())), preferred_element_type=jnp.float32
        )
        square = right.astype(jnp.float32)
        square = square * square
        folded = square[:, :128]
        for lane in range(128, square.shape[1], 128):
            folded = folded + square[:, lane : lane + 128]
        power = jnp.sum(folded.T, axis=0, keepdims=True)
        inv_b = lax.rsqrt(power / square.shape[1] + EPS)
        spot = pl.ds(tile * TILE, TILE)
        noisy = gumbel[step, :, spot].astype(jnp.float32)
        value = jnp.exp(cross * inv_a[...] * inv_b + noisy)
        plan[:, pl.ds(pl.multiple_of(step * width + tile * TILE, TILE), TILE)] = value
        total[:rows, :] += value[:, :128] + value[:, 128:]

    @pl.when(step == pl.num_programs(0) - 1)
    def _():
        mass[...] = across(total)[:, :rows]


def make_plan(near, ours, gumbel):
    rows, columns = gumbel.shape
    share, count = ours[0].shape
    width = columns // 4
    place = jnp.stack(
        [lax.axis_index("y"), lax.axis_index("x"), lax.axis_index(COL), lax.axis_index("core")]
    ).astype(jnp.int32)
    return pl.pallas_call(
        plan_kernel,
        grid_spec=pltpu.PrefetchScalarGridSpec(
            num_scalar_prefetch=1,
            grid=(4,),
            in_specs=[pl.BlockSpec(memory_space=pl.ANY)] * 12
            + [pl.BlockSpec(memory_space=pltpu.HBM)],
            out_specs=[
                pl.BlockSpec(memory_space=pltpu.VMEM),
                pl.BlockSpec((1, rows), lambda i, p: (0, 0)),
            ],
            scratch_shapes=[
                pltpu.VMEM((4, 4, 4, share, count), jnp.bfloat16),
                pltpu.VMEM((4, share, count), jnp.bfloat16),
                pltpu.VMEM((4, rows, width), jnp.bfloat16),
                pltpu.VMEM((rows, 1), jnp.float32),
                pltpu.VMEM((padded(rows), 128), jnp.float32),
                pltpu.SemaphoreType.DMA((4, 4)),
                pltpu.SemaphoreType.DMA((4,)),
                pltpu.SemaphoreType.DMA((4,)),
            ],
        ),
        out_shape=[
            pltpu.VMEM((rows, columns), jnp.float32),
            jax.ShapeDtypeStruct((1, rows), jnp.float32),
        ],
        compiler_params=pltpu.CompilerParams(
            dimension_semantics=("arbitrary",), vmem_limit_bytes=26 * 1024 * 1024
        ),
        cost_estimate=pl.CostEstimate(
            flops=2 * rows * columns * count,
            bytes_accessed=rows * columns * 6 + columns * count * 2,
            transcendentals=rows * columns,
        ),
    )(place, *pinned(near, pltpu.VMEM), *ours, *pinned([gumbel]))


def local(stream_a, stream_b, up_a, up_b, gumbel):
    share, depth = stream_a.shape
    up_a = up_a.T.reshape(2, 2, -1, depth)
    up_b = up_b.transpose(1, 2, 0).reshape(2, 2, -1, depth)

    which = lax.broadcasted_iota(jnp.int32, (2, share, depth), 0)
    near = shifted(jnp.where(which == 0, stream_b[None], stream_a[None]), "zh")
    near = [in_order([v[i] for v in near], "zh").reshape(-1, depth) for i in range(2)]
    near = late_gather(early_gather(jnp.stack(near, axis=0))[0])
    mine, other = project(near, up_a, up_b)
    near = swapped(other, "core")
    keep, give = mine[0] + near[0], mine[1] + near[1]
    act_b = (keep[0] + swapped(give[0], "zl")).astype(jnp.bfloat16)
    near = in_order(shifted(act_b, "zh"), "zh")
    near, away_a = early_gather(near, give[1])
    act_a = (keep[1] + away_a).astype(jnp.bfloat16)
    ours = crossed(act_a, COL)
    near = late_gather(near)

    plan, row_mass = make_plan(near, ours, gumbel)
    for step in range(ITERS):
        if step > 0:
            row_mass = row_sums(plan, hid_sum(col_mass))
        row_mass = sum(crossed(row_mass, COL))
        col_mass = col_sums(plan, row_mass)
    return (-jnp.log(row_mass[0]), -jnp.log(hid_share(col_mass)))


def solution(mesh):
    fine = Mesh(mesh.devices.reshape(4, 4, 4, 2, 2), HID + COL)
    placed = (
        P(HID, COL),
        P(HID, COL),
        P(COL, HID),
        P(COL, None, HID),
        P(HID, COL),
    )
    return jax.shard_map(
        local, mesh=fine, in_specs=placed, out_specs=(P(HID), P(COL, HID)), check_vma=False
    )
```

```python
import jax
import jax.numpy as jnp
from jax import lax
from jax.experimental import pallas as pl
from jax.experimental.pallas import tpu as pltpu
from jax.sharding import Mesh, PartitionSpec as P

ITERS = 3


EPS = 1e-06
SHARPNESS = 32.0

HID = ("y", "zh", "x")
COL = ("zl", "core")
TILE = 256


def shifted(value, axis):
    near = {0: value}
    for shift in (2, 1, 3):
        near[shift] = lax.ppermute(value, axis, [(i, (i + shift) % 4) for i in range(4)])
    return [near[shift] for shift in range(4)]


def crossed(value, axes):
    size = lax.axis_size(axes)
    return [value] + [
        lax.ppermute(value, axes, [(i, i ^ flip) for i in range(size)]) for flip in range(1, size)
    ]


def pinned(values, space=pltpu.HBM):
    return [pltpu.with_memory_space_constraint(value, space) for value in values]


def across_chips(value, shift, early):
    pairs = []
    for y in range(4):
        for x in range(4):
            for core in range(2):
                if (core == 0) == early:
                    to = (4 * y + (x + shift) % 4) * 2 + core
                else:
                    to = (4 * ((y + shift) % 4) + x) * 2 + core
                pairs.append(((4 * y + x) * 2 + core, to))
    return lax.ppermute(value, ("y", "x", "core"), pairs)


def early_gather(value, give=None):
    value, give = lax.optimization_barrier((value, give))
    near = [value] + [across_chips(value, shift, True) for shift in (1, 2, 3)]
    got = None if give is None else swapped(give, "zl")
    near = lax.optimization_barrier(near)
    me = jnp.where(lax.axis_index("core") == 0, lax.axis_index("x"), lax.axis_index("y"))
    return (placed(near, me, (0, 1)), placed(near, me, (2, 3))), got


def fetch_kernel(*refs):
    count = len(refs) // 2
    sem = refs[-1]
    moves = [
        pltpu.make_async_copy(refs[i], refs[count + i], sem.at[i]) for i in range(count)
    ]
    for move in moves:
        move.start()
    for move in moves:
        move.wait()


def fetched(values):
    size = sum(value.size * 2 for value in values)
    return pl.pallas_call(
        fetch_kernel,
        in_specs=[pl.BlockSpec(memory_space=pltpu.HBM)] * len(values),
        out_specs=[pl.BlockSpec(memory_space=pltpu.VMEM)] * len(values),
        out_shape=[pltpu.VMEM(value.shape, value.dtype) for value in values],
        scratch_shapes=[pltpu.SemaphoreType.DMA((len(values),))],
        compiler_params=pltpu.CompilerParams(vmem_limit_bytes=1024 * 1024),
        cost_estimate=pl.CostEstimate(flops=0, bytes_accessed=size, transcendentals=0),
    )(*pinned(values))


def late_gather(halves, extra):
    (low, high), extra = lax.optimization_barrier((halves, extra))
    low_back = across_chips(low, 1, False)
    high_ahead = across_chips(high, 3, False)
    high_back = across_chips(high, 1, False)
    low_ahead = across_chips(low, 3, False)
    extra = fetched(extra)
    low_away = across_chips(low_back, 1, False)
    high_away = across_chips(high_ahead, 3, False)
    return lax.optimization_barrier(
        (
            [low, high, low_back, high_back, low_away, high_away, low_ahead, high_ahead],
            extra,
        )
    )


def hid_sum(value):
    for axis in ("x", "zh", "y"):
        value = sum(shifted(value, axis))
    return value


def hid_share(value):
    parts = value.reshape(lax.axis_size(HID), -1)
    return jnp.sum(lax.all_to_all(parts, HID, 0, 0, tiled=True), axis=0, keepdims=True)


def placed(near, me, spots):
    size = len(near)
    return jnp.stack(
        [lax.select_n((me - spot + size) % size, *near) for spot in spots], axis=0
    )


def in_order(near, axis):
    return placed(near, lax.axis_index(axis), range(len(near)))


def project_kernel(place, *refs):
    near = refs[0:8]
    weights_a, weights_b, mine, other, held_a, held_b, sem = refs[8:]
    y, x, zl, core = (place[i] for i in range(4))
    rows, cols = [], []
    for slot, held in enumerate((held_b, held_a)):
        for i in range(8):
            at_y = lax.rem(y - i // 2 + 4, 4)
            at_x = lax.rem(x - i // 2 + 4, 4)
            source, spot = near[i].at[:, slot], pl.ds(2 * (i % 2), 2)
            signal = sem.at[8 * slot + i]
            rows.append(pltpu.make_async_copy(source, held.at[at_y, spot], signal))
            cols.append(pltpu.make_async_copy(source, held.at[spot, at_x], signal))
    @pl.when(core == 0)
    def _():
        for move in rows:
            move.start()

    @pl.when(core == 1)
    def _():
        for move in cols:
            move.start()

    depth = held_a.shape[-1]
    for slot, held, weights in ((0, held_b, weights_b), (1, held_a, weights_a)):
        for move in rows[8 * slot : 8 * slot + 8]:
            move.wait()
        tokens = held[...].reshape(-1, depth)
        for out, which in ((other, 1 - core), (mine, core)):
            part = jnp.stack([weights[zl, which], weights[1 - zl, which]], axis=0)
            found = lax.dot_general(
                part.reshape(-1, depth),
                tokens,
                (((1,), (1,)), ((), ())),
                preferred_element_type=jnp.float32,
            )
            out[:, slot] = found.reshape(2, -1, found.shape[1])


def project(near, weights_a, weights_b):
    _, _, width, depth = weights_a.shape
    rows = near[0].shape[2]
    count = 16 * rows
    place = jnp.stack([lax.axis_index(axis) for axis in ("y", "x", "zl", "core")]).astype(jnp.int32)
    inside = pl.BlockSpec(memory_space=pltpu.VMEM)
    out = jax.ShapeDtypeStruct((2, 2, width, count), jnp.float32)
    return pl.pallas_call(
        project_kernel,
        in_specs=[pl.BlockSpec(memory_space=pltpu.SMEM)]
        + [pl.BlockSpec(memory_space=pl.ANY)] * 8
        + [inside] * 2,
        out_specs=[inside, inside],
        scratch_shapes=[
            pltpu.VMEM((4, 4, rows, depth), jnp.bfloat16),
            pltpu.VMEM((4, 4, rows, depth), jnp.bfloat16),
            pltpu.SemaphoreType.DMA((16,)),
        ],
        out_shape=[out, out],
        compiler_params=pltpu.CompilerParams(vmem_limit_bytes=12 * 1024 * 1024),
        cost_estimate=pl.CostEstimate(
            flops=2 * 8 * width * depth * count,
            bytes_accessed=(8 * width + 2 * count) * depth * 2,
            transcendentals=0,
        ),
    )(place, *near, *pinned([weights_a, weights_b], pltpu.VMEM))


def swapped(value, axis):
    return lax.ppermute(value, axis, [(0, 1), (1, 0)])


def padded(rows):
    return -(-rows // 128) * 128


def across(total):
    return jnp.sum(total[...].T, axis=0, keepdims=True)


def row_kernel(plan, col_mass, mass, scale, total):
    rows, columns = plan.shape
    scale[...] = 1.0 / col_mass[...]
    total[...] = jnp.zeros_like(total)

    def body(block, carry):
        spot = pl.ds(pl.multiple_of(block * 64, 64), 64)
        found = jnp.zeros((64, 128), jnp.float32)
        for lane in range(0, columns, 128):
            found = found + plan[spot, lane : lane + 128] * scale[:, lane : lane + 128]
        total[spot, :] = found
        return carry

    lax.fori_loop(0, rows // 64, body, 0)
    mass[...] = across(total)[:, :rows]


def col_kernel(plan, row_mass, mass, scale, wide):
    rows, columns = plan.shape
    scale[...] = jnp.ones_like(scale)
    scale[:, :rows] = 1.0 / row_mass[...]
    wide[...] = jnp.broadcast_to(scale[...], (128, scale.shape[1])).T

    def body(block, carry):
        spot = pl.ds(pl.multiple_of(block * 1024, 1024), 1024)
        found = jnp.zeros((8, 1024), jnp.float32)
        for row in range(0, rows, 8):
            factor = jnp.concatenate([wide[row : row + 8, :]] * 8, axis=1)
            found = found + plan[row : row + 8, spot] * factor
        mass[:, spot] = jnp.sum(found, axis=0, keepdims=True)
        return carry

    lax.fori_loop(0, columns // 1024, body, 0)


def plan_pass(kernel, plan, mass, width, scratch):
    inside = pl.BlockSpec(memory_space=pltpu.VMEM)
    return pl.pallas_call(
        kernel,
        in_specs=[inside, inside],
        out_specs=inside,
        out_shape=jax.ShapeDtypeStruct((1, width), jnp.float32),
        scratch_shapes=[pltpu.VMEM(shape, jnp.float32) for shape in scratch],
        compiler_params=pltpu.CompilerParams(vmem_limit_bytes=4 * 1024 * 1024),
        cost_estimate=pl.CostEstimate(
            flops=2 * plan.size, bytes_accessed=4 * plan.size, transcendentals=0
        ),
    )(pltpu.with_memory_space_constraint(plan, pltpu.VMEM), mass)


def row_sums(plan, col_mass):
    rows, columns = plan.shape
    return plan_pass(row_kernel, plan, col_mass, rows, [(1, columns), (padded(rows), 128)])


def col_sums(plan, row_mass):
    rows, columns = plan.shape
    return plan_pass(
        col_kernel, plan, row_mass, columns, [(1, padded(rows)), (padded(rows), 128)]
    )


def plan_kernel(place, *refs):
    near, ours = refs[0:8], refs[8:12]
    gumbel, plan, mass, held_b, held_a, inv_a, total, sem_b, sem_a = refs[12:]
    step = pl.program_id(0)
    rows, columns = plan.shape
    width = columns // 4
    y, x, c, core = (place[i] for i in range(4))

    def block_move(source, at_y, at_x):
        return pltpu.make_async_copy(source, held_b.at[at_y, :, at_x], sem_b.at[at_y, at_x])

    @pl.when(step == 0)
    def _():
        moves = [
            pltpu.make_async_copy(ours[flip], held_a.at[c ^ flip], sem_a.at[flip])
            for flip in range(4)
        ]
        by_row, by_col = [], []
        for i in range(8):
            at_y = lax.rem(y - i // 2 + 4, 4)
            at_x = lax.rem(x - i // 2 + 4, 4)
            for spot in range(2):
                line = 2 * (i % 2) + spot
                by_row.append(block_move(near[i].at[spot], at_y, line))
                by_col.append((line, block_move(near[i].at[spot], line, at_x)))
        for move in moves:
            move.start()

        @pl.when(core == 0)
        def _():
            for move in by_row:
                move.start()

        @pl.when(core == 1)
        def _():
            for _, move in sorted(by_col, key=lambda pair: pair[0]):
                move.start()

        for move in moves:
            move.wait()
        values = held_a[...].reshape(rows, -1).astype(jnp.float32)
        scale = SHARPNESS / values.shape[1]
        inv_a[...] = scale * lax.rsqrt(jnp.mean(values * values, axis=1, keepdims=True) + EPS)
        total[...] = jnp.zeros_like(total)

    for line in range(4):
        block_move(near[0].at[0], step, line).wait()
    left = held_a[...].reshape(rows, -1)
    flat = held_b.reshape(4 * width, left.shape[1])
    for tile in range(width // TILE):
        right = flat[pl.ds(pl.multiple_of(step * width + tile * TILE, TILE), TILE), :]
        cross = lax.dot_general(
            left, right, (((1,), (1,)), ((), ())), preferred_element_type=jnp.float32
        )
        square = right.astype(jnp.float32)
        square = square * square
        folded = square[:, :128]
        for lane in range(128, square.shape[1], 128):
            folded = folded + square[:, lane : lane + 128]
        power = jnp.sum(folded.T, axis=0, keepdims=True)
        inv_b = lax.rsqrt(power / square.shape[1] + EPS)
        spot = pl.ds(pl.multiple_of(step * width + tile * TILE, TILE), TILE)
        noisy = gumbel[:, spot].astype(jnp.float32)
        value = jnp.exp(cross * inv_a[...] * inv_b + noisy)
        plan[:, spot] = value
        total[:rows, :] += value[:, :128] + value[:, 128:]

    @pl.when(step == pl.num_programs(0) - 1)
    def _():
        mass[...] = across(total)[:, :rows]


def make_plan(near, ours, gumbel):
    rows, columns = gumbel.shape
    share, count = ours[0].shape
    width = columns // 4
    place = jnp.stack(
        [lax.axis_index("y"), lax.axis_index("x"), lax.axis_index(COL), lax.axis_index("core")]
    ).astype(jnp.int32)
    return pl.pallas_call(
        plan_kernel,
        grid_spec=pltpu.PrefetchScalarGridSpec(
            num_scalar_prefetch=1,
            grid=(4,),
            in_specs=[pl.BlockSpec(memory_space=pl.ANY)] * 12
            + [pl.BlockSpec(memory_space=pltpu.VMEM)],
            out_specs=[
                pl.BlockSpec(memory_space=pltpu.VMEM),
                pl.BlockSpec((1, rows), lambda i, p: (0, 0)),
            ],
            scratch_shapes=[
                pltpu.VMEM((4, 4, 4, share, count), jnp.bfloat16),
                pltpu.VMEM((4, share, count), jnp.bfloat16),
                pltpu.VMEM((rows, 1), jnp.float32),
                pltpu.VMEM((padded(rows), 128), jnp.float32),
                pltpu.SemaphoreType.DMA((4, 4)),
                pltpu.SemaphoreType.DMA((4,)),
            ],
        ),
        out_shape=[
            pltpu.VMEM((rows, columns), jnp.float32),
            jax.ShapeDtypeStruct((1, rows), jnp.float32),
        ],
        compiler_params=pltpu.CompilerParams(
            dimension_semantics=("arbitrary",), vmem_limit_bytes=14 * 1024 * 1024
        ),
        cost_estimate=pl.CostEstimate(
            flops=2 * rows * columns * count,
            bytes_accessed=rows * columns * 6 + columns * count * 2,
            transcendentals=rows * columns,
        ),
    )(place, *pinned(near, pltpu.VMEM), *ours, *pinned([gumbel], pltpu.VMEM))


def local(stream_a, stream_b, up_a, up_b, gumbel):
    share, depth = stream_a.shape
    up_a = up_a.T.reshape(2, 2, -1, depth)
    up_b = up_b.transpose(1, 2, 0).reshape(2, 2, -1, depth)

    which = lax.broadcasted_iota(jnp.int32, (2, share, depth), 0)
    near = shifted(jnp.where(which == 0, stream_b[None], stream_a[None]), "zh")
    near = [in_order([v[i] for v in near], "zh").reshape(-1, depth) for i in range(2)]
    near, (up_a, up_b) = late_gather(early_gather(jnp.stack(near, axis=0))[0], [up_a, up_b])
    mine, other = project(near, up_a, up_b)
    near = swapped(other, "core")
    keep, give = mine[0] + near[0], mine[1] + near[1]
    act_b = (keep[0] + swapped(give[0], "zl")).astype(jnp.bfloat16)
    near = in_order(shifted(act_b, "zh"), "zh")
    near, away_a = early_gather(near, give[1])
    act_a = (keep[1] + away_a).astype(jnp.bfloat16)
    ours = crossed(act_a, COL)
    near, (gumbel,) = late_gather(near, [gumbel])

    plan, row_mass = make_plan(near, ours, gumbel)
    for step in range(ITERS):
        if step > 0:
            row_mass = row_sums(plan, hid_sum(col_mass))
        row_mass = sum(crossed(row_mass, COL))
        col_mass = col_sums(plan, row_mass)
    return (-jnp.log(row_mass[0]), -jnp.log(hid_share(col_mass)))


def solution(mesh):
    fine = Mesh(mesh.devices.reshape(4, 4, 4, 2, 2), HID + COL)
    placed = (
        P(HID, COL),
        P(HID, COL),
        P(COL, HID),
        P(COL, None, HID),
        P(HID, COL),
    )
    return jax.shard_map(
        local, mesh=fine, in_specs=placed, out_specs=(P(HID), P(COL, HID)), check_vma=False
    )
```

```python
import jax
import jax.numpy as jnp
from jax import lax
from jax.experimental import pallas as pl
from jax.experimental.pallas import tpu as pltpu
from jax.sharding import Mesh, PartitionSpec as P

ITERS = 3


EPS = 1e-06
SHARPNESS = 32.0

HID = ("y", "zh", "x")
COL = ("zl", "core")
TILE = 256


def shifted(value, axis):
    back, away, ahead = (
        lax.ppermute(value, axis, [(i, (i + shift) % 4) for i in range(4)]) for shift in (1, 2, 3)
    )
    return [value, back, away, ahead]


def ended(near):
    value, back, away, ahead = near
    ahead, back, away, value = lax.optimization_barrier((ahead, back, away, value))
    return [value, back, away, ahead]


def crossed(value, axes):
    size = lax.axis_size(axes)
    return [value] + [
        lax.ppermute(value, axes, [(i, i ^ flip) for i in range(size)]) for flip in range(1, size)
    ]


def pinned(values, space=pltpu.HBM):
    return [pltpu.with_memory_space_constraint(value, space) for value in values]


def across_chips(value, shift, early):
    pairs = []
    for y in range(4):
        for x in range(4):
            for core in range(2):
                if (core == 0) == early:
                    to = (4 * y + (x + shift) % 4) * 2 + core
                else:
                    to = (4 * ((y + shift) % 4) + x) * 2 + core
                pairs.append(((4 * y + x) * 2 + core, to))
    return lax.ppermute(value, ("y", "x", "core"), pairs)


def early_gather(value, give=None):
    value, give = lax.optimization_barrier((value, give))
    near = ended([value] + [across_chips(value, shift, True) for shift in (1, 2, 3)])
    got = None if give is None else swapped(give, "zl")
    me = jnp.where(lax.axis_index("core") == 0, lax.axis_index("x"), lax.axis_index("y"))
    return (placed(near, me, (0, 1)), placed(near, me, (2, 3))), got


def fetch_kernel(*refs):
    count = len(refs) // 2
    sem = refs[-1]
    moves = [
        pltpu.make_async_copy(refs[i], refs[count + i], sem.at[i]) for i in range(count)
    ]
    for move in moves:
        move.start()
    for move in moves:
        move.wait()


def fetched(values):
    size = sum(value.size * 2 for value in values)
    return pl.pallas_call(
        fetch_kernel,
        in_specs=[pl.BlockSpec(memory_space=pltpu.HBM)] * len(values),
        out_specs=[pl.BlockSpec(memory_space=pltpu.VMEM)] * len(values),
        out_shape=[pltpu.VMEM(value.shape, value.dtype) for value in values],
        scratch_shapes=[pltpu.SemaphoreType.DMA((len(values),))],
        compiler_params=pltpu.CompilerParams(vmem_limit_bytes=1024 * 1024),
        cost_estimate=pl.CostEstimate(flops=0, bytes_accessed=size, transcendentals=0),
    )(*pinned(values))


def late_gather(halves, extra):
    (low, high), extra = lax.optimization_barrier((halves, extra))
    low_back = across_chips(low, 1, False)
    high_ahead = across_chips(high, 3, False)
    high_back = across_chips(high, 1, False)
    low_ahead = across_chips(low, 3, False)
    extra = fetched(extra)
    low_away = across_chips(low_back, 1, False)
    high_away = across_chips(high_ahead, 3, False)
    return lax.optimization_barrier(
        (
            [low, high, low_back, high_back, low_away, high_away, low_ahead, high_ahead],
            extra,
        )
    )


def hid_sum(value):
    for axis in ("x", "zh", "y"):
        value, back, away, ahead = shifted(value, axis)
        value = value + ahead + back + away
    return value


def hid_share(parts):
    return jnp.sum(lax.all_to_all(parts, HID, 0, 0, tiled=True), axis=0, keepdims=True)


def placed(near, me, spots):
    size = len(near)
    return jnp.stack(
        [lax.select_n((me - spot + size) % size, *near) for spot in spots], axis=0
    )


def in_order(near, axis):
    return placed(near, lax.axis_index(axis), range(len(near)))


def project_kernel(place, *refs):
    near = refs[0:8]
    weights_a, weights_b, mine, other, held_a, held_b, sem = refs[8:]
    y, x, zl, core = (place[i] for i in range(4))
    rows, cols = [], []
    for slot, held in enumerate((held_b, held_a)):
        for i in range(8):
            at_y = lax.rem(y - i // 2 + 4, 4)
            at_x = lax.rem(x - i // 2 + 4, 4)
            source, spot = near[i].at[:, slot], pl.ds(2 * (i % 2), 2)
            signal = sem.at[8 * slot + i]
            rows.append(pltpu.make_async_copy(source, held.at[at_y, spot], signal))
            cols.append(pltpu.make_async_copy(source, held.at[spot, at_x], signal))
    @pl.when(core == 0)
    def _():
        for move in rows:
            move.start()

    @pl.when(core == 1)
    def _():
        for move in cols:
            move.start()

    depth = held_a.shape[-1]
    for slot, held, weights in ((0, held_b, weights_b), (1, held_a, weights_a)):
        for move in rows[8 * slot : 8 * slot + 8]:
            move.wait()
        tokens = held[...].reshape(-1, depth)
        for out, which in ((other, 1 - core), (mine, core)):
            part = jnp.stack([weights[zl, which], weights[1 - zl, which]], axis=0)
            found = lax.dot_general(
                part.reshape(-1, depth),
                tokens,
                (((1,), (1,)), ((), ())),
                preferred_element_type=jnp.float32,
            )
            out[:, slot] = found.reshape(2, -1, found.shape[1])


def project(near, weights_a, weights_b):
    _, _, width, depth = weights_a.shape
    rows = near[0].shape[2]
    count = 16 * rows
    place = jnp.stack([lax.axis_index(axis) for axis in ("y", "x", "zl", "core")]).astype(jnp.int32)
    inside = pl.BlockSpec(memory_space=pltpu.VMEM)
    out = jax.ShapeDtypeStruct((2, 2, width, count), jnp.float32)
    return pl.pallas_call(
        project_kernel,
        in_specs=[pl.BlockSpec(memory_space=pltpu.SMEM)]
        + [pl.BlockSpec(memory_space=pl.ANY)] * 8
        + [inside] * 2,
        out_specs=[inside, inside],
        scratch_shapes=[
            pltpu.VMEM((4, 4, rows, depth), jnp.bfloat16),
            pltpu.VMEM((4, 4, rows, depth), jnp.bfloat16),
            pltpu.SemaphoreType.DMA((16,)),
        ],
        out_shape=[out, out],
        compiler_params=pltpu.CompilerParams(vmem_limit_bytes=12 * 1024 * 1024),
        cost_estimate=pl.CostEstimate(
            flops=2 * 8 * width * depth * count,
            bytes_accessed=(8 * width + 2 * count) * depth * 2,
            transcendentals=0,
        ),
    )(place, *near, *pinned([weights_a, weights_b], pltpu.VMEM))


def swapped(value, axis):
    return lax.ppermute(value, axis, [(0, 1), (1, 0)])


def padded(rows):
    return -(-rows // 128) * 128


def across(total):
    return jnp.sum(total[...].T, axis=0, keepdims=True)


def row_kernel(plan, col_mass, mass, scale, total):
    rows, columns = plan.shape
    scale[...] = 1.0 / col_mass[...]
    total[...] = jnp.zeros_like(total)

    def body(block, carry):
        spot = pl.ds(pl.multiple_of(block * 64, 64), 64)
        found = jnp.zeros((64, 128), jnp.float32)
        for lane in range(0, columns, 128):
            found = found + plan[spot, lane : lane + 128] * scale[:, lane : lane + 128]
        total[spot, :] = found
        return carry

    lax.fori_loop(0, rows // 64, body, 0)
    mass[...] = across(total)[:, :rows]


def col_kernel(plan, row_mass, mass, scale, wide):
    rows, columns = plan.shape
    scale[...] = jnp.ones_like(scale)
    scale[:, :rows] = 1.0 / row_mass[...]
    wide[...] = jnp.broadcast_to(scale[...], (128, scale.shape[1])).T

    def body(block, carry):
        spot = pl.ds(pl.multiple_of(block * 1024, 1024), 1024)
        found = jnp.zeros((8, 1024), jnp.float32)
        for row in range(0, rows, 8):
            factor = jnp.concatenate([wide[row : row + 8, :]] * 8, axis=1)
            found = found + plan[row : row + 8, spot] * factor
        mass[:, spot] = jnp.sum(found, axis=0, keepdims=True)
        return carry

    lax.fori_loop(0, columns // 1024, body, 0)


def share_kernel(plan, row_mass, mass, scale, wide, whole):
    col_kernel(plan, row_mass, whole, scale, wide)
    parts = mass.shape[0]
    share = whole.shape[1] // parts
    mass[...] = jnp.zeros_like(mass)
    for part in range(parts):
        mass[part : part + 1, :share] = whole[:, part * share : (part + 1) * share]


def plan_pass(kernel, plan, mass, shape, scratch):
    inside = pl.BlockSpec(memory_space=pltpu.VMEM)
    return pl.pallas_call(
        kernel,
        in_specs=[inside, inside],
        out_specs=inside,
        out_shape=jax.ShapeDtypeStruct(shape, jnp.float32),
        scratch_shapes=[pltpu.VMEM(size, jnp.float32) for size in scratch],
        compiler_params=pltpu.CompilerParams(vmem_limit_bytes=4 * 1024 * 1024),
        cost_estimate=pl.CostEstimate(
            flops=2 * plan.size, bytes_accessed=4 * plan.size, transcendentals=0
        ),
    )(pltpu.with_memory_space_constraint(plan, pltpu.VMEM), mass)


def row_sums(plan, col_mass):
    rows, columns = plan.shape
    return plan_pass(row_kernel, plan, col_mass, (1, rows), [(1, columns), (padded(rows), 128)])


def col_sums(plan, row_mass):
    rows, columns = plan.shape
    scratch = [(1, padded(rows)), (padded(rows), 128)]
    return plan_pass(col_kernel, plan, row_mass, (1, columns), scratch)


def col_sums_by_share(plan, row_mass):
    rows, columns = plan.shape
    parts = lax.axis_size(HID)
    scratch = [(1, padded(rows)), (padded(rows), 128), (1, columns)]
    shape = (parts, padded(columns // parts))
    return plan_pass(share_kernel, plan, row_mass, shape, scratch)


def plan_kernel(place, *refs):
    near, ours = refs[0:8], refs[8:12]
    gumbel, plan, mass, held_b, held_a, inv_a, total, sem_b, sem_a = refs[12:]
    step = pl.program_id(0)
    rows, columns = plan.shape
    width = columns // 4
    y, x, c, core = (place[i] for i in range(4))

    def block_move(source, at_y, at_x):
        return pltpu.make_async_copy(source, held_b.at[at_y, :, at_x], sem_b.at[at_y, at_x])

    @pl.when(step == 0)
    def _():
        moves = [
            pltpu.make_async_copy(ours[flip], held_a.at[c ^ flip], sem_a.at[flip])
            for flip in range(4)
        ]
        by_row, by_col = [], []
        for i in range(8):
            at_y = lax.rem(y - i // 2 + 4, 4)
            at_x = lax.rem(x - i // 2 + 4, 4)
            for spot in range(2):
                line = 2 * (i % 2) + spot
                by_row.append(block_move(near[i].at[spot], at_y, line))
                by_col.append((line, block_move(near[i].at[spot], line, at_x)))
        for move in moves:
            move.start()

        @pl.when(core == 0)
        def _():
            for move in by_row:
                move.start()

        @pl.when(core == 1)
        def _():
            for _, move in sorted(by_col, key=lambda pair: pair[0]):
                move.start()

        for move in moves:
            move.wait()
        values = held_a[...].reshape(rows, -1).astype(jnp.float32)
        scale = SHARPNESS / values.shape[1]
        unit = scale * lax.rsqrt(jnp.mean(values * values, axis=1, keepdims=True) + EPS)
        inv_a[...] = jnp.broadcast_to(unit, inv_a.shape)
        total[...] = jnp.zeros_like(total)

    block = jnp.where(core == 0, lax.rem(y - step + 4, 4), step)
    for line in range(4):
        block_move(near[0].at[0], block, line).wait()
    left = held_a[...].reshape(rows, -1)
    flat = held_b.reshape(4 * width, left.shape[1])
    for tile in range(width // TILE):
        right = flat[pl.ds(pl.multiple_of(block * width + tile * TILE, TILE), TILE), :]
        cross = lax.dot_general(
            left, right, (((1,), (1,)), ((), ())), preferred_element_type=jnp.float32
        )
        square = right.astype(jnp.float32)
        square = square * square
        folded = square[:, :128]
        for lane in range(128, square.shape[1], 128):
            folded = folded + square[:, lane : lane + 128]
        power = jnp.sum(folded.T, axis=0, keepdims=True)
        inv_b = lax.rsqrt(power / square.shape[1] + EPS)
        spot = pl.ds(pl.multiple_of(block * width + tile * TILE, TILE), TILE)
        noisy = gumbel[:, spot].astype(jnp.float32)
        value = jnp.exp(cross * inv_a[...] * inv_b + noisy)
        plan[:, spot] = value
        total[:rows, :] += value[:, :128] + value[:, 128:]

    @pl.when(step == pl.num_programs(0) - 1)
    def _():
        mass[...] = across(total)[:, :rows]


def make_plan(near, ours, gumbel):
    rows, columns = gumbel.shape
    share, count = ours[0].shape
    width = columns // 4
    place = jnp.stack(
        [lax.axis_index("y"), lax.axis_index("x"), lax.axis_index(COL), lax.axis_index("core")]
    ).astype(jnp.int32)
    return pl.pallas_call(
        plan_kernel,
        grid_spec=pltpu.PrefetchScalarGridSpec(
            num_scalar_prefetch=1,
            grid=(4,),
            in_specs=[pl.BlockSpec(memory_space=pl.ANY)] * 12
            + [pl.BlockSpec(memory_space=pltpu.VMEM)],
            out_specs=[
                pl.BlockSpec(memory_space=pltpu.VMEM),
                pl.BlockSpec((1, rows), lambda i, p: (0, 0)),
            ],
            scratch_shapes=[
                pltpu.VMEM((4, 4, 4, share, count), jnp.bfloat16),
                pltpu.VMEM((4, share, count), jnp.bfloat16),
                pltpu.VMEM((rows, TILE), jnp.float32),
                pltpu.VMEM((padded(rows), 128), jnp.float32),
                pltpu.SemaphoreType.DMA((4, 4)),
                pltpu.SemaphoreType.DMA((4,)),
            ],
        ),
        out_shape=[
            pltpu.VMEM((rows, columns), jnp.float32),
            jax.ShapeDtypeStruct((1, rows), jnp.float32),
        ],
        compiler_params=pltpu.CompilerParams(
            dimension_semantics=("arbitrary",), vmem_limit_bytes=14 * 1024 * 1024
        ),
        cost_estimate=pl.CostEstimate(
            flops=2 * rows * columns * count,
            bytes_accessed=rows * columns * 6 + columns * count * 2,
            transcendentals=rows * columns,
        ),
    )(place, *pinned(near, pltpu.VMEM), *ours, *pinned([gumbel], pltpu.VMEM))


def local(stream_a, stream_b, up_a, up_b, gumbel):
    share, depth = stream_a.shape
    up_a = up_a.T.reshape(2, 2, -1, depth)
    up_b = up_b.transpose(1, 2, 0).reshape(2, 2, -1, depth)

    which = lax.broadcasted_iota(jnp.int32, (2, share, depth), 0)
    near = ended(shifted(jnp.where(which == 0, stream_b[None], stream_a[None]), "zh"))
    near = [in_order([v[i] for v in near], "zh").reshape(-1, depth) for i in range(2)]
    near, (up_a, up_b) = late_gather(early_gather(jnp.stack(near, axis=0))[0], [up_a, up_b])
    mine, other = project(near, up_a, up_b)
    near = swapped(other, "core")
    keep, give = mine[0] + near[0], mine[1] + near[1]
    act_b = (keep[0] + swapped(give[0], "zl")).astype(jnp.bfloat16)
    near = in_order(ended(shifted(act_b, "zh")), "zh")
    near, away_a = early_gather(near, give[1])
    act_a = (keep[1] + away_a).astype(jnp.bfloat16)
    ours = crossed(act_a, COL)
    near, (gumbel,) = late_gather(near, [gumbel])

    plan, row_mass = make_plan(near, ours, gumbel)
    for step in range(ITERS):
        if step > 0:
            row_mass = row_sums(plan, hid_sum(col_mass))
        row_mass = sum(crossed(row_mass, COL))
        if step < ITERS - 1:
            col_mass = col_sums(plan, row_mass)
    share = gumbel.shape[1] // lax.axis_size(HID)
    own = hid_share(col_sums_by_share(plan, row_mass))[:, :share]
    return (-jnp.log(row_mass[0]), -jnp.log(own))


def solution(mesh):
    fine = Mesh(mesh.devices.reshape(4, 4, 4, 2, 2), HID + COL)
    placed = (
        P(HID, COL),
        P(HID, COL),
        P(COL, HID),
        P(COL, None, HID),
        P(HID, COL),
    )
    return jax.shard_map(
        local, mesh=fine, in_specs=placed, out_specs=(P(HID), P(COL, HID)), check_vma=False
    )
```

```python
import functools

import jax
import jax.numpy as jnp
from jax import lax
from jax.experimental import pallas as pl
from jax.experimental.pallas import tpu as pltpu
from jax.sharding import Mesh, PartitionSpec as P

ITERS = 3


EPS = 1e-06
SHARPNESS = 32.0

HID = ("y", "zh", "x")
COL = ("zl", "core")
TILE = 256


def shifted(value, axis):
    back, away, ahead = (
        lax.ppermute(value, axis, [(i, (i + shift) % 4) for i in range(4)]) for shift in (1, 2, 3)
    )
    return [value, back, away, ahead]


def ended(near):
    value, back, away, ahead = near
    ahead, back, away, value = lax.optimization_barrier((ahead, back, away, value))
    return [value, back, away, ahead]


def crossed(value, axes):
    size = lax.axis_size(axes)
    return [value] + [
        lax.ppermute(value, axes, [(i, i ^ flip) for i in range(size)]) for flip in range(1, size)
    ]


def pinned(values, space=pltpu.HBM):
    return [pltpu.with_memory_space_constraint(value, space) for value in values]


def across_chips(value, shift, early):
    pairs = []
    for y in range(4):
        for x in range(4):
            for core in range(2):
                if (core == 0) == early:
                    to = (4 * y + (x + shift) % 4) * 2 + core
                else:
                    to = (4 * ((y + shift) % 4) + x) * 2 + core
                pairs.append(((4 * y + x) * 2 + core, to))
    return lax.ppermute(value, ("y", "x", "core"), pairs)


def early_gather(value, give=None):
    value, give = lax.optimization_barrier((value, give))
    near = ended([value] + [across_chips(value, shift, True) for shift in (1, 2, 3)])
    got = None if give is None else swapped(give, "zl")
    me = jnp.where(lax.axis_index("core") == 0, lax.axis_index("x"), lax.axis_index("y"))
    return (placed(near, me, (0, 1)), placed(near, me, (2, 3))), got


def fetch_kernel(*refs):
    count = len(refs) // 2
    sem = refs[-1]
    moves = [
        pltpu.make_async_copy(refs[i], refs[count + i], sem.at[i]) for i in range(count)
    ]
    for move in moves:
        move.start()
    for move in moves:
        move.wait()


def fetched(values):
    size = sum(value.size * 2 for value in values)
    return pl.pallas_call(
        fetch_kernel,
        in_specs=[pl.BlockSpec(memory_space=pltpu.HBM)] * len(values),
        out_specs=[pl.BlockSpec(memory_space=pltpu.VMEM)] * len(values),
        out_shape=[pltpu.VMEM(value.shape, value.dtype) for value in values],
        scratch_shapes=[pltpu.SemaphoreType.DMA((len(values),))],
        compiler_params=pltpu.CompilerParams(vmem_limit_bytes=1024 * 1024),
        cost_estimate=pl.CostEstimate(flops=0, bytes_accessed=size, transcendentals=0),
    )(*pinned(values))


def late_gather(halves, extra):
    (low, high), extra = lax.optimization_barrier((halves, extra))
    low_back = across_chips(low, 1, False)
    high_ahead = across_chips(high, 3, False)
    high_back = across_chips(high, 1, False)
    low_ahead = across_chips(low, 3, False)
    extra = fetched(extra)
    low_away = across_chips(low_back, 1, False)
    high_away = across_chips(high_ahead, 3, False)
    return lax.optimization_barrier(
        (
            [low, high, low_back, high_back, low_away, high_away, low_ahead, high_ahead],
            extra,
        )
    )


def hid_sum(value):
    for axis in ("x", "zh", "y"):
        value, back, away, ahead = shifted(value, axis)
        value = value + ahead + back + away
    return value


def hid_share(parts):
    return jnp.sum(lax.all_to_all(parts, HID, 0, 0, tiled=True), axis=0, keepdims=True)


def placed(near, me, spots, way=1):
    size = len(near)
    return jnp.stack(
        [lax.select_n(((me - spot) * way + size) % size, *near) for spot in spots], axis=0
    )


def in_order(near, axis, way=1):
    return placed(near, lax.axis_index(axis), range(len(near)), way)


def spun(value, axis):
    ahead = [(2 * i + c, 2 * ((i + 1 - 2 * c) % 4) + c) for i in range(4) for c in (0, 1)]
    behind = [(to, by) for by, to in ahead]
    one = lax.ppermute(value, (axis, "core"), ahead)
    three = lax.ppermute(value, (axis, "core"), behind)
    two = lax.ppermute(one, (axis, "core"), ahead)
    return [value, one, two, three], 1 - 2 * lax.axis_index("core")


def project_kernel(slot, place, *refs):
    near = refs[0:8]
    weights, mine, other, held, sem = refs[8:]
    y, x, zl, core = (place[i] for i in range(4))
    rows, cols = [], []
    for i in range(8):
        at_y = lax.rem(y - i // 2 + 4, 4)
        at_x = lax.rem(x - i // 2 + 4, 4)
        source, spot = near[i].at[:, slot], pl.ds(2 * (i % 2), 2)
        rows.append(pltpu.make_async_copy(source, held.at[at_y, spot], sem.at[i]))
        cols.append(pltpu.make_async_copy(source, held.at[spot, at_x], sem.at[i]))

    @pl.when(core == 0)
    def _():
        for move in rows:
            move.start()

    @pl.when(core == 1)
    def _():
        for move in cols:
            move.start()

    for move in rows:
        move.wait()
    depth = held.shape[-1]
    tokens = held[...].reshape(-1, depth)
    for out, which in ((other, 1 - core), (mine, core)):
        part = jnp.stack([weights[zl, which], weights[1 - zl, which]], axis=0)
        found = lax.dot_general(
            part.reshape(-1, depth),
            tokens,
            (((1,), (1,)), ((), ())),
            preferred_element_type=jnp.float32,
        )
        out[...] = found.reshape(2, -1, found.shape[1])


def project(near, weights, slot):
    _, _, width, depth = weights.shape
    rows = near[0].shape[2]
    count = 16 * rows
    place = jnp.stack([lax.axis_index(axis) for axis in ("y", "x", "zl", "core")]).astype(jnp.int32)
    inside = pl.BlockSpec(memory_space=pltpu.VMEM)
    out = jax.ShapeDtypeStruct((2, width, count), jnp.float32)
    return pl.pallas_call(
        functools.partial(project_kernel, slot),
        in_specs=[pl.BlockSpec(memory_space=pltpu.SMEM)]
        + [pl.BlockSpec(memory_space=pl.ANY)] * 8
        + [inside],
        out_specs=[inside, inside],
        scratch_shapes=[
            pltpu.VMEM((4, 4, rows, depth), jnp.bfloat16),
            pltpu.SemaphoreType.DMA((8,)),
        ],
        out_shape=[out, out],
        compiler_params=pltpu.CompilerParams(vmem_limit_bytes=12 * 1024 * 1024),
        cost_estimate=pl.CostEstimate(
            flops=2 * 4 * width * depth * count,
            bytes_accessed=(4 * width + count) * depth * 2,
            transcendentals=0,
        ),
    )(place, *near, *pinned([weights], pltpu.VMEM))


def core_sum(mine, other):
    near = swapped(other, "core")
    return mine[0] + near[0], mine[1] + near[1]


def swapped(value, axis):
    return lax.ppermute(value, axis, [(0, 1), (1, 0)])


def padded(rows):
    return -(-rows // 128) * 128


def across(total):
    return jnp.sum(total[...].T, axis=0, keepdims=True)


def row_kernel(plan, col_mass, mass, scale, total):
    rows, columns = plan.shape
    scale[...] = 1.0 / col_mass[...]
    total[...] = jnp.zeros_like(total)

    def body(block, carry):
        spot = pl.ds(pl.multiple_of(block * 64, 64), 64)
        found = jnp.zeros((64, 128), jnp.float32)
        for lane in range(0, columns, 128):
            found = found + plan[spot, lane : lane + 128] * scale[:, lane : lane + 128]
        total[spot, :] = found
        return carry

    lax.fori_loop(0, rows // 64, body, 0)
    mass[...] = across(total)[:, :rows]


def col_kernel(plan, row_mass, mass, scale, wide):
    rows, columns = plan.shape
    scale[...] = jnp.ones_like(scale)
    scale[:, :rows] = 1.0 / row_mass[...]
    wide[...] = jnp.broadcast_to(scale[...], (128, scale.shape[1])).T

    def body(block, carry):
        spot = pl.ds(pl.multiple_of(block * 1024, 1024), 1024)
        found = jnp.zeros((8, 1024), jnp.float32)
        for row in range(0, rows, 8):
            factor = jnp.concatenate([wide[row : row + 8, :]] * 8, axis=1)
            found = found + plan[row : row + 8, spot] * factor
        mass[:, spot] = jnp.sum(found, axis=0, keepdims=True)
        return carry

    lax.fori_loop(0, columns // 1024, body, 0)


def share_kernel(plan, row_mass, mass, scale, wide, whole):
    col_kernel(plan, row_mass, whole, scale, wide)
    parts = mass.shape[0]
    share = whole.shape[1] // parts
    mass[...] = jnp.zeros_like(mass)
    for part in range(parts):
        mass[part : part + 1, :share] = whole[:, part * share : (part + 1) * share]


def plan_pass(kernel, plan, mass, shape, scratch):
    inside = pl.BlockSpec(memory_space=pltpu.VMEM)
    return pl.pallas_call(
        kernel,
        in_specs=[inside, inside],
        out_specs=inside,
        out_shape=jax.ShapeDtypeStruct(shape, jnp.float32),
        scratch_shapes=[pltpu.VMEM(size, jnp.float32) for size in scratch],
        compiler_params=pltpu.CompilerParams(vmem_limit_bytes=4 * 1024 * 1024),
        cost_estimate=pl.CostEstimate(
            flops=2 * plan.size, bytes_accessed=4 * plan.size, transcendentals=0
        ),
    )(pltpu.with_memory_space_constraint(plan, pltpu.VMEM), mass)


def row_sums(plan, col_mass):
    rows, columns = plan.shape
    return plan_pass(row_kernel, plan, col_mass, (1, rows), [(1, columns), (padded(rows), 128)])


def col_sums(plan, row_mass):
    rows, columns = plan.shape
    scratch = [(1, padded(rows)), (padded(rows), 128)]
    return plan_pass(col_kernel, plan, row_mass, (1, columns), scratch)


def col_sums_by_share(plan, row_mass):
    rows, columns = plan.shape
    parts = lax.axis_size(HID)
    scratch = [(1, padded(rows)), (padded(rows), 128), (1, columns)]
    shape = (parts, padded(columns // parts))
    return plan_pass(share_kernel, plan, row_mass, shape, scratch)


def plan_kernel(place, *refs):
    near, ours = refs[0:8], refs[8:12]
    gumbel, plan, mass, held_b, held_a, inv_a, total, sem_b, sem_a = refs[12:]
    step = pl.program_id(0)
    rows, columns = plan.shape
    width = columns // 4
    y, x, c, core = (place[i] for i in range(4))

    def block_move(source, at_y, at_x):
        return pltpu.make_async_copy(source, held_b.at[at_y, :, at_x], sem_b.at[at_y, at_x])

    @pl.when(step == 0)
    def _():
        moves = [
            pltpu.make_async_copy(ours[flip], held_a.at[c ^ flip], sem_a.at[flip])
            for flip in range(4)
        ]
        by_row, by_col = [], []
        for i in range(8):
            at_y = lax.rem(y - i // 2 + 4, 4)
            at_x = lax.rem(x - i // 2 + 4, 4)
            for spot in range(2):
                line = 2 * (i % 2) + spot
                by_row.append(block_move(near[i].at[spot], at_y, line))
                by_col.append((line, block_move(near[i].at[spot], line, at_x)))
        for move in moves:
            move.start()

        @pl.when(core == 0)
        def _():
            for move in by_row:
                move.start()

        @pl.when(core == 1)
        def _():
            for _, move in sorted(by_col, key=lambda pair: pair[0]):
                move.start()

        for move in moves:
            move.wait()
        values = held_a[...].reshape(rows, -1).astype(jnp.float32)
        scale = SHARPNESS / values.shape[1]
        unit = scale * lax.rsqrt(jnp.mean(values * values, axis=1, keepdims=True) + EPS)
        inv_a[...] = jnp.broadcast_to(unit, inv_a.shape)
        total[...] = jnp.zeros_like(total)

    block = jnp.where(core == 0, lax.rem(y - step + 4, 4), step)
    for line in range(4):
        block_move(near[0].at[0], block, line).wait()
    left = held_a[...].reshape(rows, -1)
    flat = held_b.reshape(4 * width, left.shape[1])
    for tile in range(width // TILE):
        right = flat[pl.ds(pl.multiple_of(block * width + tile * TILE, TILE), TILE), :]
        cross = lax.dot_general(
            left, right, (((1,), (1,)), ((), ())), preferred_element_type=jnp.float32
        )
        square = right.astype(jnp.float32)
        square = square * square
        folded = square[:, :128]
        for lane in range(128, square.shape[1], 128):
            folded = folded + square[:, lane : lane + 128]
        power = jnp.sum(folded.T, axis=0, keepdims=True)
        inv_b = lax.rsqrt(power / square.shape[1] + EPS)
        spot = pl.ds(pl.multiple_of(block * width + tile * TILE, TILE), TILE)
        noisy = gumbel[:, spot].astype(jnp.float32)
        value = jnp.exp(cross * inv_a[...] * inv_b + noisy)
        plan[:, spot] = value
        total[:rows, :] += value[:, :128] + value[:, 128:]

    @pl.when(step == pl.num_programs(0) - 1)
    def _():
        mass[...] = across(total)[:, :rows]


def make_plan(near, ours, gumbel):
    rows, columns = gumbel.shape
    share, count = ours[0].shape
    width = columns // 4
    place = jnp.stack(
        [lax.axis_index("y"), lax.axis_index("x"), lax.axis_index(COL), lax.axis_index("core")]
    ).astype(jnp.int32)
    return pl.pallas_call(
        plan_kernel,
        grid_spec=pltpu.PrefetchScalarGridSpec(
            num_scalar_prefetch=1,
            grid=(4,),
            in_specs=[pl.BlockSpec(memory_space=pl.ANY)] * 12
            + [pl.BlockSpec(memory_space=pltpu.VMEM)],
            out_specs=[
                pl.BlockSpec(memory_space=pltpu.VMEM),
                pl.BlockSpec((1, rows), lambda i, p: (0, 0)),
            ],
            scratch_shapes=[
                pltpu.VMEM((4, 4, 4, share, count), jnp.bfloat16),
                pltpu.VMEM((4, share, count), jnp.bfloat16),
                pltpu.VMEM((rows, TILE), jnp.float32),
                pltpu.VMEM((padded(rows), 128), jnp.float32),
                pltpu.SemaphoreType.DMA((4, 4)),
                pltpu.SemaphoreType.DMA((4,)),
            ],
        ),
        out_shape=[
            pltpu.VMEM((rows, columns), jnp.float32),
            jax.ShapeDtypeStruct((1, rows), jnp.float32),
        ],
        compiler_params=pltpu.CompilerParams(
            dimension_semantics=("arbitrary",), vmem_limit_bytes=14 * 1024 * 1024
        ),
        cost_estimate=pl.CostEstimate(
            flops=2 * rows * columns * count,
            bytes_accessed=rows * columns * 6 + columns * count * 2,
            transcendentals=rows * columns,
        ),
    )(place, *pinned(near, pltpu.VMEM), *ours, *pinned([gumbel], pltpu.VMEM))


def local(stream_a, stream_b, up_a, up_b, gumbel):
    share, depth = stream_a.shape
    up_a = up_a.T.reshape(2, 2, -1, depth)
    up_b = up_b.transpose(1, 2, 0).reshape(2, 2, -1, depth)

    which = lax.broadcasted_iota(jnp.int32, (2, share, depth), 0)
    near = ended(shifted(jnp.where(which == 0, stream_b[None], stream_a[None]), "zh"))
    near = [in_order([v[i] for v in near], "zh").reshape(-1, depth) for i in range(2)]
    near, (up_a, up_b) = late_gather(early_gather(jnp.stack(near, axis=0))[0], [up_a, up_b])
    keep_b, give_b = core_sum(*project(near, up_b, 0))
    give_b, near = lax.optimization_barrier((give_b, near))
    act_b = (keep_b + swapped(give_b, "zl")).astype(jnp.bfloat16)
    keep_a, give_a = core_sum(*project(near, up_a, 1))
    act_b, give_a = lax.optimization_barrier((act_b, give_a))
    near, way = spun(act_b, "zh")
    near = in_order(lax.optimization_barrier(near), "zh", way)
    near, away_a = early_gather(near, give_a)
    act_a = (keep_a + away_a).astype(jnp.bfloat16)
    ours = crossed(act_a, COL)
    near, (gumbel,) = late_gather(near, [gumbel])

    plan, row_mass = make_plan(near, ours, gumbel)
    for step in range(ITERS):
        if step > 0:
            row_mass = row_sums(plan, hid_sum(col_mass))
        row_mass = sum(crossed(row_mass, COL))
        if step < ITERS - 1:
            col_mass = col_sums(plan, row_mass)
    share = gumbel.shape[1] // lax.axis_size(HID)
    own = hid_share(col_sums_by_share(plan, row_mass))[:, :share]
    return (-jnp.log(row_mass[0]), -jnp.log(own))


def solution(mesh):
    fine = Mesh(mesh.devices.reshape(4, 4, 4, 2, 2), HID + COL)
    placed = (
        P(HID, COL),
        P(HID, COL),
        P(COL, HID),
        P(COL, None, HID),
        P(HID, COL),
    )
    return jax.shard_map(
        local, mesh=fine, in_specs=placed, out_specs=(P(HID), P(COL, HID)), check_vma=False
    )
```

```python
import functools

import jax
import jax.numpy as jnp
from jax import lax
from jax.experimental import pallas as pl
from jax.experimental.pallas import tpu as pltpu
from jax.sharding import Mesh, PartitionSpec as P

ITERS = 3


EPS = 1e-06
SHARPNESS = 32.0

HID = ("y", "zh", "x")
COL = ("zl", "core")
TILE = 256


def shifted(value, axis):
    back, away, ahead = (
        lax.ppermute(value, axis, [(i, (i + shift) % 4) for i in range(4)]) for shift in (1, 2, 3)
    )
    return [value, back, away, ahead]


def ended(near):
    value, back, away, ahead = near
    ahead, back, away, value = lax.optimization_barrier((ahead, back, away, value))
    return [value, back, away, ahead]


def crossed(value, axes):
    size = lax.axis_size(axes)
    return [value] + [
        lax.ppermute(value, axes, [(i, i ^ flip) for i in range(size)]) for flip in range(1, size)
    ]


def pinned(values, space=pltpu.HBM):
    return [pltpu.with_memory_space_constraint(value, space) for value in values]


def across_chips(value, shift, early):
    pairs = []
    for y in range(4):
        for x in range(4):
            for core in range(2):
                if (core == 0) == early:
                    to = (4 * y + (x + shift) % 4) * 2 + core
                else:
                    to = (4 * ((y + shift) % 4) + x) * 2 + core
                pairs.append(((4 * y + x) * 2 + core, to))
    return lax.ppermute(value, ("y", "x", "core"), pairs)


def early_gather(value, give=None):
    value, give = lax.optimization_barrier((value, give))
    near = ended([value] + [across_chips(value, shift, True) for shift in (1, 2, 3)])
    got = None if give is None else swapped(give, "zl")
    me = jnp.where(lax.axis_index("core") == 0, lax.axis_index("x"), lax.axis_index("y"))
    return (placed(near, me, (0, 1)), placed(near, me, (2, 3))), got


def fetch_kernel(*refs):
    count = len(refs) // 2
    sem = refs[-1]
    moves = [
        pltpu.make_async_copy(refs[i], refs[count + i], sem.at[i]) for i in range(count)
    ]
    for move in moves:
        move.start()
    for move in moves:
        move.wait()


def fetched(values):
    size = sum(value.size * 2 for value in values)
    return pl.pallas_call(
        fetch_kernel,
        in_specs=[pl.BlockSpec(memory_space=pltpu.HBM)] * len(values),
        out_specs=[pl.BlockSpec(memory_space=pltpu.VMEM)] * len(values),
        out_shape=[pltpu.VMEM(value.shape, value.dtype) for value in values],
        scratch_shapes=[pltpu.SemaphoreType.DMA((len(values),))],
        compiler_params=pltpu.CompilerParams(vmem_limit_bytes=1024 * 1024),
        cost_estimate=pl.CostEstimate(flops=0, bytes_accessed=size, transcendentals=0),
    )(*pinned(values))


def late_gather(halves, extra):
    (low, high), extra = lax.optimization_barrier((halves, extra))
    low_back = across_chips(low, 1, False)
    high_ahead = across_chips(high, 3, False)
    high_back = across_chips(high, 1, False)
    low_ahead = across_chips(low, 3, False)
    extra = fetched(extra)
    low_away = across_chips(low_back, 1, False)
    high_away = across_chips(high_ahead, 3, False)
    return lax.optimization_barrier(
        (
            [low, high, low_back, high_back, low_away, high_away, low_ahead, high_ahead],
            extra,
        )
    )


def hid_sum(value):
    for axis in ("x", "zh", "y"):
        value, back, away, ahead = shifted(value, axis)
        value = value + ahead + back + away
    return value


def hid_share(parts):
    return jnp.sum(lax.all_to_all(parts, HID, 0, 0, tiled=True), axis=0, keepdims=True)


def placed(near, me, spots):
    size = len(near)
    return jnp.stack(
        [lax.select_n((me - spot + size) % size, *near) for spot in spots], axis=0
    )


def in_order(near, axis):
    return placed(near, lax.axis_index(axis), range(len(near)))


def project_kernel(slot, place, *refs):
    near = refs[0:8]
    weights, mine, other, held, sem = refs[8:]
    y, x, zl, core = (place[i] for i in range(4))
    rows, cols = [], []
    for i in range(8):
        at_y = lax.rem(y - i // 2 + 4, 4)
        at_x = lax.rem(x - i // 2 + 4, 4)
        source, spot = near[i].at[:, slot], pl.ds(2 * (i % 2), 2)
        rows.append(pltpu.make_async_copy(source, held.at[at_y, spot], sem.at[i]))
        cols.append(pltpu.make_async_copy(source, held.at[spot, at_x], sem.at[i]))

    @pl.when(core == 0)
    def _():
        for move in rows:
            move.start()

    @pl.when(core == 1)
    def _():
        for move in cols:
            move.start()

    for move in rows:
        move.wait()
    depth = held.shape[-1]
    tokens = held[...].reshape(-1, depth)
    for out, which in ((other, 1 - core), (mine, core)):
        part = jnp.stack([weights[zl, which], weights[1 - zl, which]], axis=0)
        found = lax.dot_general(
            part.reshape(-1, depth),
            tokens,
            (((1,), (1,)), ((), ())),
            preferred_element_type=jnp.float32,
        )
        out[...] = found.reshape(2, -1, found.shape[1])


def project(near, weights, slot):
    _, _, width, depth = weights.shape
    rows = near[0].shape[2]
    count = 16 * rows
    place = jnp.stack([lax.axis_index(axis) for axis in ("y", "x", "zl", "core")]).astype(jnp.int32)
    inside = pl.BlockSpec(memory_space=pltpu.VMEM)
    out = jax.ShapeDtypeStruct((2, width, count), jnp.float32)
    return pl.pallas_call(
        functools.partial(project_kernel, slot),
        in_specs=[pl.BlockSpec(memory_space=pltpu.SMEM)]
        + [pl.BlockSpec(memory_space=pl.ANY)] * 8
        + [inside],
        out_specs=[inside, inside],
        scratch_shapes=[
            pltpu.VMEM((4, 4, rows, depth), jnp.bfloat16),
            pltpu.SemaphoreType.DMA((8,)),
        ],
        out_shape=[out, out],
        compiler_params=pltpu.CompilerParams(vmem_limit_bytes=12 * 1024 * 1024),
        cost_estimate=pl.CostEstimate(
            flops=2 * 4 * width * depth * count,
            bytes_accessed=(4 * width + count) * depth * 2,
            transcendentals=0,
        ),
    )(place, *near, *pinned([weights], pltpu.VMEM))


def core_sum(mine, other):
    near = swapped(other, "core")
    return mine[0] + near[0], mine[1] + near[1]


def swapped(value, axis):
    return lax.ppermute(value, axis, [(0, 1), (1, 0)])


def padded(rows):
    return -(-rows // 128) * 128


def across(total):
    return jnp.sum(total[...].T, axis=0, keepdims=True)


def row_kernel(plan, col_mass, mass, scale, total):
    rows, columns = plan.shape
    scale[...] = 1.0 / col_mass[...]
    total[...] = jnp.zeros_like(total)

    def body(block, carry):
        spot = pl.ds(pl.multiple_of(block * 64, 64), 64)
        found = jnp.zeros((64, 128), jnp.float32)
        for lane in range(0, columns, 128):
            found = found + plan[spot, lane : lane + 128] * scale[:, lane : lane + 128]
        total[spot, :] = found
        return carry

    lax.fori_loop(0, rows // 64, body, 0)
    mass[...] = across(total)[:, :rows]


def col_kernel(plan, row_mass, mass, scale, wide):
    rows, columns = plan.shape
    scale[...] = jnp.ones_like(scale)
    scale[:, :rows] = 1.0 / row_mass[...]
    wide[...] = jnp.broadcast_to(scale[...], (128, scale.shape[1])).T

    def body(block, carry):
        spot = pl.ds(pl.multiple_of(block * 1024, 1024), 1024)
        found = jnp.zeros((8, 1024), jnp.float32)
        for row in range(0, rows, 8):
            factor = jnp.concatenate([wide[row : row + 8, :]] * 8, axis=1)
            found = found + plan[row : row + 8, spot] * factor
        mass[:, spot] = jnp.sum(found, axis=0, keepdims=True)
        return carry

    lax.fori_loop(0, columns // 1024, body, 0)


def share_kernel(plan, row_mass, mass, scale, wide, whole):
    col_kernel(plan, row_mass, whole, scale, wide)
    parts = mass.shape[0]
    share = whole.shape[1] // parts
    mass[...] = jnp.zeros_like(mass)
    for part in range(parts):
        mass[part : part + 1, :share] = whole[:, part * share : (part + 1) * share]


def plan_pass(kernel, plan, mass, shape, scratch):
    inside = pl.BlockSpec(memory_space=pltpu.VMEM)
    return pl.pallas_call(
        kernel,
        in_specs=[inside, inside],
        out_specs=inside,
        out_shape=jax.ShapeDtypeStruct(shape, jnp.float32),
        scratch_shapes=[pltpu.VMEM(size, jnp.float32) for size in scratch],
        compiler_params=pltpu.CompilerParams(vmem_limit_bytes=4 * 1024 * 1024),
        cost_estimate=pl.CostEstimate(
            flops=2 * plan.size, bytes_accessed=4 * plan.size, transcendentals=0
        ),
    )(pltpu.with_memory_space_constraint(plan, pltpu.VMEM), mass)


def row_sums(plan, col_mass):
    rows, columns = plan.shape
    return plan_pass(row_kernel, plan, col_mass, (1, rows), [(1, columns), (padded(rows), 128)])


def col_sums(plan, row_mass):
    rows, columns = plan.shape
    scratch = [(1, padded(rows)), (padded(rows), 128)]
    return plan_pass(col_kernel, plan, row_mass, (1, columns), scratch)


def col_sums_by_share(plan, row_mass):
    rows, columns = plan.shape
    parts = lax.axis_size(HID)
    scratch = [(1, padded(rows)), (padded(rows), 128), (1, columns)]
    shape = (parts, padded(columns // parts))
    return plan_pass(share_kernel, plan, row_mass, shape, scratch)


def plan_kernel(place, *refs):
    near, ours = refs[0:8], refs[8:12]
    gumbel, plan, mass, held_b, held_a, inv_a, total, sem_b, sem_a = refs[12:]
    step = pl.program_id(0)
    rows, columns = plan.shape
    width = columns // 4
    y, x, c, core = (place[i] for i in range(4))

    def block_move(source, at_y, at_x):
        return pltpu.make_async_copy(source, held_b.at[at_y, :, at_x], sem_b.at[at_y, at_x])

    @pl.when(step == 0)
    def _():
        moves = [
            pltpu.make_async_copy(ours[flip], held_a.at[c ^ flip], sem_a.at[flip])
            for flip in range(4)
        ]
        by_row, by_col = [], []
        for i in range(8):
            at_y = lax.rem(y - i // 2 + 4, 4)
            at_x = lax.rem(x - i // 2 + 4, 4)
            for spot in range(2):
                line = 2 * (i % 2) + spot
                by_row.append(block_move(near[i].at[spot], at_y, line))
                by_col.append((line, block_move(near[i].at[spot], line, at_x)))
        for move in moves:
            move.start()

        @pl.when(core == 0)
        def _():
            for move in by_row:
                move.start()

        @pl.when(core == 1)
        def _():
            for _, move in sorted(by_col, key=lambda pair: pair[0]):
                move.start()

        for move in moves:
            move.wait()
        values = held_a[...].reshape(rows, -1).astype(jnp.float32)
        scale = SHARPNESS / values.shape[1]
        unit = scale * lax.rsqrt(jnp.mean(values * values, axis=1, keepdims=True) + EPS)
        inv_a[...] = jnp.broadcast_to(unit, inv_a.shape)
        total[...] = jnp.zeros_like(total)

    block = jnp.where(core == 0, lax.rem(y - step + 4, 4), step)
    for line in range(4):
        block_move(near[0].at[0], block, line).wait()
    left = held_a[...].reshape(rows, -1)
    flat = held_b.reshape(4 * width, left.shape[1])
    for tile in range(width // TILE):
        right = flat[pl.ds(pl.multiple_of(block * width + tile * TILE, TILE), TILE), :]
        cross = lax.dot_general(
            left, right, (((1,), (1,)), ((), ())), preferred_element_type=jnp.float32
        )
        square = right.astype(jnp.float32)
        square = square * square
        folded = square[:, :128]
        for lane in range(128, square.shape[1], 128):
            folded = folded + square[:, lane : lane + 128]
        power = jnp.sum(folded.T, axis=0, keepdims=True)
        inv_b = lax.rsqrt(power / square.shape[1] + EPS)
        spot = pl.ds(pl.multiple_of(block * width + tile * TILE, TILE), TILE)
        noisy = gumbel[:, spot].astype(jnp.float32)
        value = jnp.exp(cross * inv_a[...] * inv_b + noisy)
        plan[:, spot] = value
        total[:rows, :] += value[:, :128] + value[:, 128:]

    @pl.when(step == pl.num_programs(0) - 1)
    def _():
        mass[...] = across(total)[:, :rows]


def make_plan(near, ours, gumbel):
    rows, columns = gumbel.shape
    share, count = ours[0].shape
    width = columns // 4
    place = jnp.stack(
        [lax.axis_index("y"), lax.axis_index("x"), lax.axis_index(COL), lax.axis_index("core")]
    ).astype(jnp.int32)
    return pl.pallas_call(
        plan_kernel,
        grid_spec=pltpu.PrefetchScalarGridSpec(
            num_scalar_prefetch=1,
            grid=(4,),
            in_specs=[pl.BlockSpec(memory_space=pl.ANY)] * 12
            + [pl.BlockSpec(memory_space=pltpu.VMEM)],
            out_specs=[
                pl.BlockSpec(memory_space=pltpu.VMEM),
                pl.BlockSpec((1, rows), lambda i, p: (0, 0)),
            ],
            scratch_shapes=[
                pltpu.VMEM((4, 4, 4, share, count), jnp.bfloat16),
                pltpu.VMEM((4, share, count), jnp.bfloat16),
                pltpu.VMEM((rows, TILE), jnp.float32),
                pltpu.VMEM((padded(rows), 128), jnp.float32),
                pltpu.SemaphoreType.DMA((4, 4)),
                pltpu.SemaphoreType.DMA((4,)),
            ],
        ),
        out_shape=[
            pltpu.VMEM((rows, columns), jnp.float32),
            jax.ShapeDtypeStruct((1, rows), jnp.float32),
        ],
        compiler_params=pltpu.CompilerParams(
            dimension_semantics=("arbitrary",), vmem_limit_bytes=14 * 1024 * 1024
        ),
        cost_estimate=pl.CostEstimate(
            flops=2 * rows * columns * count,
            bytes_accessed=rows * columns * 6 + columns * count * 2,
            transcendentals=rows * columns,
        ),
    )(place, *pinned(near, pltpu.VMEM), *ours, *pinned([gumbel], pltpu.VMEM))


def local(stream_a, stream_b, up_a, up_b, gumbel):
    share, depth = stream_a.shape
    up_a = up_a.T.reshape(2, 2, -1, depth)
    up_b = up_b.transpose(1, 2, 0).reshape(2, 2, -1, depth)

    which = lax.broadcasted_iota(jnp.int32, (2, share, depth), 0)
    near = ended(shifted(jnp.where(which == 0, stream_b[None], stream_a[None]), "zh"))
    near = [in_order([v[i] for v in near], "zh").reshape(-1, depth) for i in range(2)]
    near, (up_a, up_b) = late_gather(early_gather(jnp.stack(near, axis=0))[0], [up_a, up_b])
    keep_b, give_b = core_sum(*project(near, up_b, 0))
    give_b, near = lax.optimization_barrier((give_b, near))
    act_b = (keep_b + swapped(give_b, "zl")).astype(jnp.bfloat16)
    keep_a, give_a = core_sum(*project(near, up_a, 1))
    act_b, give_a = lax.optimization_barrier((act_b, give_a))
    near = in_order(ended(shifted(act_b, "zh")), "zh")
    near, away_a = early_gather(near, give_a)
    act_a = (keep_a + away_a).astype(jnp.bfloat16)
    ours = crossed(act_a, COL)
    near, (gumbel,) = late_gather(near, [gumbel])

    plan, row_mass = make_plan(near, ours, gumbel)
    for step in range(ITERS):
        if step > 0:
            row_mass = row_sums(plan, hid_sum(col_mass))
        row_mass = sum(crossed(row_mass, COL))
        if step < ITERS - 1:
            col_mass = col_sums(plan, row_mass)
    share = gumbel.shape[1] // lax.axis_size(HID)
    own = hid_share(col_sums_by_share(plan, row_mass))[:, :share]
    return (-jnp.log(row_mass[0]), -jnp.log(own))


def solution(mesh):
    fine = Mesh(mesh.devices.reshape(4, 4, 4, 2, 2), HID + COL)
    placed = (
        P(HID, COL),
        P(HID, COL),
        P(COL, HID),
        P(COL, None, HID),
        P(HID, COL),
    )
    return jax.shard_map(
        local, mesh=fine, in_specs=placed, out_specs=(P(HID), P(COL, HID)), check_vma=False
    )
```

```python
import functools

import jax
import jax.numpy as jnp
from jax import lax
from jax.experimental import pallas as pl
from jax.experimental.pallas import tpu as pltpu
from jax.sharding import Mesh, PartitionSpec as P

ITERS = 3


EPS = 1e-06
SHARPNESS = 32.0

HID = ("y", "zh", "x")
COL = ("zl", "core")
TILE = 256


def shifted(value, axis):
    back, away, ahead = (
        lax.ppermute(value, axis, [(i, (i + shift) % 4) for i in range(4)]) for shift in (1, 2, 3)
    )
    return [value, back, away, ahead]


def ended(near):
    value, back, away, ahead = near
    ahead, back, away, value = lax.optimization_barrier((ahead, back, away, value))
    return [value, back, away, ahead]


def crossed(value, axes):
    size = lax.axis_size(axes)
    return [value] + [
        lax.ppermute(value, axes, [(i, i ^ flip) for i in range(size)]) for flip in range(1, size)
    ]


def pinned(values, space=pltpu.HBM):
    return [pltpu.with_memory_space_constraint(value, space) for value in values]


def across_chips(value, shift, early):
    pairs = []
    for y in range(4):
        for x in range(4):
            for core in range(2):
                if (core == 0) == early:
                    to = (4 * y + (x + shift) % 4) * 2 + core
                else:
                    to = (4 * ((y + shift) % 4) + x) * 2 + core
                pairs.append(((4 * y + x) * 2 + core, to))
    return lax.ppermute(value, ("y", "x", "core"), pairs)


def early_gather(value, give=None):
    value, give = lax.optimization_barrier((value, give))
    near = ended([value] + [across_chips(value, shift, True) for shift in (1, 2, 3)])
    got = None if give is None else swapped(give, "zl")
    me = jnp.where(lax.axis_index("core") == 0, lax.axis_index("x"), lax.axis_index("y"))
    return (placed(near, me, (0, 1)), placed(near, me, (2, 3))), got


def fetch_kernel(*refs):
    count = len(refs) // 2
    sem = refs[-1]
    moves = [
        pltpu.make_async_copy(refs[i], refs[count + i], sem.at[i]) for i in range(count)
    ]
    for move in moves:
        move.start()
    for move in moves:
        move.wait()


def fetched(values):
    size = sum(value.size * 2 for value in values)
    return pl.pallas_call(
        fetch_kernel,
        in_specs=[pl.BlockSpec(memory_space=pltpu.HBM)] * len(values),
        out_specs=[pl.BlockSpec(memory_space=pltpu.VMEM)] * len(values),
        out_shape=[pltpu.VMEM(value.shape, value.dtype) for value in values],
        scratch_shapes=[pltpu.SemaphoreType.DMA((len(values),))],
        compiler_params=pltpu.CompilerParams(vmem_limit_bytes=1024 * 1024),
        cost_estimate=pl.CostEstimate(flops=0, bytes_accessed=size, transcendentals=0),
    )(*pinned(values))


def late_gather(halves, extra):
    (low, high), extra = lax.optimization_barrier((halves, extra))
    low_back = across_chips(low, 1, False)
    high_ahead = across_chips(high, 3, False)
    high_back = across_chips(high, 1, False)
    low_ahead = across_chips(low, 3, False)
    extra = fetched(extra)
    low_away = across_chips(low_back, 1, False)
    high_away = across_chips(high_ahead, 3, False)
    return lax.optimization_barrier(
        (
            [low, high, low_back, high_back, low_away, high_away, low_ahead, high_ahead],
            extra,
        )
    )


def hid_sum(value):
    for axis in ("x", "y", "zh"):
        value, back, away, ahead = shifted(value, axis)
        value = value + ahead + back + away
    return value


def hid_share(parts):
    return jnp.sum(lax.all_to_all(parts, HID, 0, 0, tiled=True), axis=0, keepdims=True)


def placed(near, me, spots):
    size = len(near)
    return jnp.stack(
        [lax.select_n((me - spot + size) % size, *near) for spot in spots], axis=0
    )


def in_order(near, axis):
    return placed(near, lax.axis_index(axis), range(len(near)))


def project_kernel(slot, place, *refs):
    near = refs[0:8]
    weights, mine, other, held, sem = refs[8:]
    y, x, zl, core = (place[i] for i in range(4))
    rows, cols = [], []
    for i in range(8):
        at_y = lax.rem(y - i // 2 + 4, 4)
        at_x = lax.rem(x - i // 2 + 4, 4)
        source, spot = near[i].at[:, slot], pl.ds(2 * (i % 2), 2)
        rows.append(pltpu.make_async_copy(source, held.at[at_y, spot], sem.at[i]))
        cols.append(pltpu.make_async_copy(source, held.at[spot, at_x], sem.at[i]))

    @pl.when(core == 0)
    def _():
        for move in rows:
            move.start()

    @pl.when(core == 1)
    def _():
        for move in cols:
            move.start()

    for move in rows:
        move.wait()
    depth = held.shape[-1]
    tokens = held[...].reshape(-1, depth)
    for out, which in ((other, 1 - core), (mine, core)):
        part = jnp.stack([weights[zl, which], weights[1 - zl, which]], axis=0)
        found = lax.dot_general(
            part.reshape(-1, depth),
            tokens,
            (((1,), (1,)), ((), ())),
            preferred_element_type=jnp.float32,
        )
        out[...] = found.reshape(2, -1, found.shape[1])


def project(near, weights, slot):
    _, _, width, depth = weights.shape
    rows = near[0].shape[2]
    count = 16 * rows
    place = jnp.stack([lax.axis_index(axis) for axis in ("y", "x", "zl", "core")]).astype(jnp.int32)
    inside = pl.BlockSpec(memory_space=pltpu.VMEM)
    out = jax.ShapeDtypeStruct((2, width, count), jnp.float32)
    return pl.pallas_call(
        functools.partial(project_kernel, slot),
        in_specs=[pl.BlockSpec(memory_space=pltpu.SMEM)]
        + [pl.BlockSpec(memory_space=pl.ANY)] * 8
        + [inside],
        out_specs=[inside, inside],
        scratch_shapes=[
            pltpu.VMEM((4, 4, rows, depth), jnp.bfloat16),
            pltpu.SemaphoreType.DMA((8,)),
        ],
        out_shape=[out, out],
        compiler_params=pltpu.CompilerParams(vmem_limit_bytes=12 * 1024 * 1024),
        cost_estimate=pl.CostEstimate(
            flops=2 * 4 * width * depth * count,
            bytes_accessed=(4 * width + count) * depth * 2,
            transcendentals=0,
        ),
    )(place, *near, *pinned([weights], pltpu.VMEM))


def core_sum(mine, other):
    near = swapped(other, "core")
    return mine[0] + near[0], mine[1] + near[1]


def swapped(value, axis):
    return lax.ppermute(value, axis, [(0, 1), (1, 0)])


def padded(rows):
    return -(-rows // 128) * 128


def across(total):
    return jnp.sum(total[...].T, axis=0, keepdims=True)


def row_kernel(plan, col_mass, mass, scale, total):
    rows, columns = plan.shape
    scale[...] = 1.0 / col_mass[...]
    total[...] = jnp.zeros_like(total)

    def body(block, carry):
        spot = pl.ds(pl.multiple_of(block * 64, 64), 64)
        found = jnp.zeros((64, 128), jnp.float32)
        for lane in range(0, columns, 128):
            found = found + plan[spot, lane : lane + 128] * scale[:, lane : lane + 128]
        total[spot, :] = found
        return carry

    lax.fori_loop(0, rows // 64, body, 0)
    mass[...] = across(total)[:, :rows]


def col_kernel(plan, row_mass, mass, scale, wide):
    rows, columns = plan.shape
    scale[...] = jnp.ones_like(scale)
    scale[:, :rows] = 1.0 / row_mass[...]
    wide[...] = jnp.broadcast_to(scale[...], (128, scale.shape[1])).T

    def body(block, carry):
        spot = pl.ds(pl.multiple_of(block * 1024, 1024), 1024)
        found = jnp.zeros((8, 1024), jnp.float32)
        for row in range(0, rows, 8):
            factor = jnp.concatenate([wide[row : row + 8, :]] * 8, axis=1)
            found = found + plan[row : row + 8, spot] * factor
        mass[:, spot] = jnp.sum(found, axis=0, keepdims=True)
        return carry

    lax.fori_loop(0, columns // 1024, body, 0)


def share_kernel(plan, row_mass, mass, scale, wide, whole):
    col_kernel(plan, row_mass, whole, scale, wide)
    parts = mass.shape[0]
    share = whole.shape[1] // parts
    mass[...] = jnp.zeros_like(mass)
    for part in range(parts):
        mass[part : part + 1, :share] = whole[:, part * share : (part + 1) * share]


def plan_pass(kernel, plan, mass, shape, scratch):
    inside = pl.BlockSpec(memory_space=pltpu.VMEM)
    return pl.pallas_call(
        kernel,
        in_specs=[inside, inside],
        out_specs=inside,
        out_shape=jax.ShapeDtypeStruct(shape, jnp.float32),
        scratch_shapes=[pltpu.VMEM(size, jnp.float32) for size in scratch],
        compiler_params=pltpu.CompilerParams(vmem_limit_bytes=4 * 1024 * 1024),
        cost_estimate=pl.CostEstimate(
            flops=2 * plan.size, bytes_accessed=4 * plan.size, transcendentals=0
        ),
    )(pltpu.with_memory_space_constraint(plan, pltpu.VMEM), mass)


def row_sums(plan, col_mass):
    rows, columns = plan.shape
    return plan_pass(row_kernel, plan, col_mass, (1, rows), [(1, columns), (padded(rows), 128)])


def col_sums(plan, row_mass):
    rows, columns = plan.shape
    scratch = [(1, padded(rows)), (padded(rows), 128)]
    return plan_pass(col_kernel, plan, row_mass, (1, columns), scratch)


def col_sums_by_share(plan, row_mass):
    rows, columns = plan.shape
    parts = lax.axis_size(HID)
    scratch = [(1, padded(rows)), (padded(rows), 128), (1, columns)]
    shape = (parts, padded(columns // parts))
    return plan_pass(share_kernel, plan, row_mass, shape, scratch)


def plan_kernel(place, *refs):
    near, ours = refs[0:8], refs[8:12]
    gumbel, plan, mass, held_b, held_a, inv_a, total, sem_b, sem_a = refs[12:]
    step = pl.program_id(0)
    rows, columns = plan.shape
    width = columns // 4
    y, x, c, core = (place[i] for i in range(4))

    def block_move(source, at_y, at_x):
        return pltpu.make_async_copy(source, held_b.at[at_y, :, at_x], sem_b.at[at_y, at_x])

    @pl.when(step == 0)
    def _():
        moves = [
            pltpu.make_async_copy(ours[flip], held_a.at[c ^ flip], sem_a.at[flip])
            for flip in range(4)
        ]
        by_row, by_col = [], []
        for i in range(8):
            at_y = lax.rem(y - i // 2 + 4, 4)
            at_x = lax.rem(x - i // 2 + 4, 4)
            for spot in range(2):
                line = 2 * (i % 2) + spot
                by_row.append(block_move(near[i].at[spot], at_y, line))
                by_col.append((line, block_move(near[i].at[spot], line, at_x)))
        for move in moves:
            move.start()

        @pl.when(core == 0)
        def _():
            for move in by_row:
                move.start()

        @pl.when(core == 1)
        def _():
            for _, move in sorted(by_col, key=lambda pair: pair[0]):
                move.start()

        for move in moves:
            move.wait()
        values = held_a[...].reshape(rows, -1).astype(jnp.float32)
        scale = SHARPNESS / values.shape[1]
        unit = scale * lax.rsqrt(jnp.mean(values * values, axis=1, keepdims=True) + EPS)
        inv_a[...] = jnp.broadcast_to(unit, inv_a.shape)
        total[...] = jnp.zeros_like(total)

    block = jnp.where(core == 0, lax.rem(y - step + 4, 4), step)
    for line in range(4):
        block_move(near[0].at[0], block, line).wait()
    left = held_a[...].reshape(rows, -1)
    flat = held_b.reshape(4 * width, left.shape[1])
    for tile in range(width // TILE):
        right = flat[pl.ds(pl.multiple_of(block * width + tile * TILE, TILE), TILE), :]
        cross = lax.dot_general(
            left, right, (((1,), (1,)), ((), ())), preferred_element_type=jnp.float32
        )
        square = right.astype(jnp.float32)
        square = square * square
        folded = square[:, :128]
        for lane in range(128, square.shape[1], 128):
            folded = folded + square[:, lane : lane + 128]
        power = jnp.sum(folded.T, axis=0, keepdims=True)
        inv_b = lax.rsqrt(power / square.shape[1] + EPS)
        spot = pl.ds(pl.multiple_of(block * width + tile * TILE, TILE), TILE)
        noisy = gumbel[:, spot].astype(jnp.float32)
        value = jnp.exp(cross * inv_a[...] * inv_b + noisy)
        plan[:, spot] = value
        total[:rows, :] += value[:, :128] + value[:, 128:]

    @pl.when(step == pl.num_programs(0) - 1)
    def _():
        mass[...] = across(total)[:, :rows]


def make_plan(near, ours, gumbel):
    rows, columns = gumbel.shape
    share, count = ours[0].shape
    width = columns // 4
    place = jnp.stack(
        [lax.axis_index("y"), lax.axis_index("x"), lax.axis_index(COL), lax.axis_index("core")]
    ).astype(jnp.int32)
    return pl.pallas_call(
        plan_kernel,
        grid_spec=pltpu.PrefetchScalarGridSpec(
            num_scalar_prefetch=1,
            grid=(4,),
            in_specs=[pl.BlockSpec(memory_space=pl.ANY)] * 12
            + [pl.BlockSpec(memory_space=pltpu.VMEM)],
            out_specs=[
                pl.BlockSpec(memory_space=pltpu.VMEM),
                pl.BlockSpec((1, rows), lambda i, p: (0, 0)),
            ],
            scratch_shapes=[
                pltpu.VMEM((4, 4, 4, share, count), jnp.bfloat16),
                pltpu.VMEM((4, share, count), jnp.bfloat16),
                pltpu.VMEM((rows, TILE), jnp.float32),
                pltpu.VMEM((padded(rows), 128), jnp.float32),
                pltpu.SemaphoreType.DMA((4, 4)),
                pltpu.SemaphoreType.DMA((4,)),
            ],
        ),
        out_shape=[
            pltpu.VMEM((rows, columns), jnp.float32),
            jax.ShapeDtypeStruct((1, rows), jnp.float32),
        ],
        compiler_params=pltpu.CompilerParams(
            dimension_semantics=("arbitrary",), vmem_limit_bytes=14 * 1024 * 1024
        ),
        cost_estimate=pl.CostEstimate(
            flops=2 * rows * columns * count,
            bytes_accessed=rows * columns * 6 + columns * count * 2,
            transcendentals=rows * columns,
        ),
    )(place, *pinned(near, pltpu.VMEM), *ours, *pinned([gumbel], pltpu.VMEM))


def local(stream_a, stream_b, up_a, up_b, gumbel):
    share, depth = stream_a.shape
    up_a = up_a.T.reshape(2, 2, -1, depth)
    up_b = up_b.transpose(1, 2, 0).reshape(2, 2, -1, depth)

    which = lax.broadcasted_iota(jnp.int32, (2, share, depth), 0)
    near = ended(shifted(jnp.where(which == 0, stream_b[None], stream_a[None]), "zh"))
    near = [in_order([v[i] for v in near], "zh").reshape(-1, depth) for i in range(2)]
    near, (up_a, up_b) = late_gather(early_gather(jnp.stack(near, axis=0))[0], [up_a, up_b])
    keep_b, give_b = core_sum(*project(near, up_b, 0))
    give_b, near = lax.optimization_barrier((give_b, near))
    act_b = (keep_b + swapped(give_b, "zl")).astype(jnp.bfloat16)
    keep_a, give_a = core_sum(*project(near, up_a, 1))
    act_b, give_a = lax.optimization_barrier((act_b, give_a))
    near = in_order(ended(shifted(act_b, "zh")), "zh")
    near, away_a = early_gather(near, give_a)
    act_a = (keep_a + away_a).astype(jnp.bfloat16)
    ours = crossed(act_a, COL)
    near, (gumbel,) = late_gather(near, [gumbel])

    plan, row_mass = make_plan(near, ours, gumbel)
    for step in range(ITERS):
        if step > 0:
            row_mass = row_sums(plan, hid_sum(col_mass))
        row_mass = sum(crossed(row_mass, COL))
        if step < ITERS - 1:
            col_mass = col_sums(plan, row_mass)
    share = gumbel.shape[1] // lax.axis_size(HID)
    own = hid_share(col_sums_by_share(plan, row_mass))[:, :share]
    return (-jnp.log(row_mass[0]), -jnp.log(own))


def solution(mesh):
    fine = Mesh(mesh.devices.reshape(4, 4, 4, 2, 2), HID + COL)
    placed = (
        P(HID, COL),
        P(HID, COL),
        P(COL, HID),
        P(COL, None, HID),
        P(HID, COL),
    )
    return jax.shard_map(
        local, mesh=fine, in_specs=placed, out_specs=(P(HID), P(COL, HID)), check_vma=False
    )
```
